32 devices in a mesh: box: 32 (over z, y, x, core).
Axes of the slice: x: 2, y: 2, z: 4, core: 2. Of those that a mesh axis runs over, the one named last changes fastest.
Arguments:
- cell_state: float32 [64, 5, 32, 1024], P('box'), as said below
- swap_slots: int32 [32], P('box'), may hold values from 0 to 1, as said below
- neighbours: int32 [64, 3], P('box'), may hold values from -1 to 63, as said below
Outputs:
- new_state: float32 [64, 5, 32, 1024], P('box')
The draws below stay inside these ranges and needn't reach their ends.
Inputs may be any that keep to these rules, and one draw needn't show every extreme that they name: `swap_slots`: each device names one of its 2 slots. `neighbours`: after the swap, device d holds the boxes of first-dimension layer d of a domain 32 layers long and two boxes wide in the second dimension; the lower first-dimension neighbour of a slot lies on device d - 1, the upper on device d + 1, the box beside in the second dimension on device d itself; -1 marks the two ends of the first dimension. `cell_state`: density, pressure and internal energy of every cell are positive.
All inputs are finite; a program needn't handle non-finite values.
Results may differ from the reference program's by a relative error of at most 0.0003.
Values sent between devices are 32-bit elements; how exact they have to be, the bound alone decides.
A program may use at most 64 MiB of HBM per device.

```python
import math
import jax
import jax.numpy as jnp
from jax import lax

BXC = 32
BYC = 32
BZC = 32
SLOTS = 2
FIELDS = 5
GHOST = 4
RIEMANN_ITERS = 3
NBOX = 64


def layout(key):
    owners_count = NBOX // SLOTS
    sent = jax.random.randint(jax.random.fold_in(key, 11), (owners_count,), 0, SLOTS).astype(jnp.int32)
    flipped = jax.random.randint(jax.random.fold_in(key, 13), (owners_count,), 0, 2).astype(jnp.int32)
    slot_ids = jnp.arange(NBOX, dtype=jnp.int32)
    device = slot_ids // SLOTS
    within = slot_ids % SLOTS
    across = jnp.bitwise_xor(within, flipped[device])

    def where_is(layer):
        return SLOTS * layer + jnp.bitwise_xor(across, flipped[layer])
    lower = jnp.where(device > 0, where_is(jnp.maximum(device - 1, 0)), -1)
    upper = jnp.where(device < owners_count - 1, where_is(jnp.minimum(device + 1, owners_count - 1)), -1)
    beside = SLOTS * device + (1 - within)
    return (sent, jnp.stack([lower, upper, beside], axis=1).astype(jnp.int32))


def draw_swap_slots(key, part):
    return layout(jax.random.fold_in(key, 5))[0]


def draw_neighbours(key, part):
    return layout(jax.random.fold_in(key, 5))[1]


def draw_cell_state(key, part):
    shape = (NBOX, BXC, BYC, BZC)
    keys = jax.random.split(jax.random.fold_in(key, 3), 5)
    owners_count = NBOX // SLOTS
    place = (jnp.arange(NBOX, dtype=jnp.int32) // SLOTS).astype(jnp.float32) / (owners_count - 1)
    ramp = 1.0 + 2.0 * place
    density = jnp.exp(jax.random.uniform(keys[0], shape, jnp.float32, math.log(0.5), math.log(2.0)))
    velocity = 0.3 * jax.random.truncated_normal(keys[1], -2.0, 2.0, (NBOX, 3, BXC, BYC, BZC), jnp.float32)
    pressure = jnp.exp(jax.random.uniform(keys[2], shape, jnp.float32, math.log(0.5), math.log(2.0)))
    velocity = velocity * ramp[:, None, None, None, None]
    pressure = pressure * (ramp * ramp)[:, None, None, None]
    cold_energy = jax.random.uniform(keys[3], shape, jnp.float32, 0.005, 0.045)
    cold = jax.random.bernoulli(keys[4], 0.1, shape)
    pressure = jnp.where(cold, 0.1 * density * density + 0.4 * density * cold_energy, pressure)
    momentum = density[:, None] * velocity
    energy = (pressure - 0.1 * density * density) / 0.4 + 0.5 * density * jnp.sum(velocity * velocity, axis=1)
    stacked = jnp.concatenate([density[:, None], momentum, energy[:, None]], axis=1)
    return stacked.reshape((NBOX, FIELDS, BXC, BYC * BZC)).astype(jnp.float32)


def setup_inputs(seed: int = 0) -> dict:
    streams_of = jax.random.split(jax.random.key(seed), 4)
    return {
        "cell_state": draw_cell_state(jax.random.fold_in(streams_of[3], 71), 0),
        "swap_slots": draw_swap_slots(jax.random.fold_in(streams_of[3], 71), 0),
        "neighbours": draw_neighbours(jax.random.fold_in(streams_of[3], 71), 0),
    }


EOS_LINEAR = 0.4
EOS_QUAD = 0.1
COURANT = 0.4

def cut(values, start, stop, sweep_axis):
    return lax.slice_in_dim(values, start, stop, axis=sweep_axis)

def minmod(first, second):
    return 0.5 * (jnp.sign(first) + jnp.sign(second)) * jnp.minimum(jnp.abs(first), jnp.abs(second))

def primitives(conserved):
    density = jnp.maximum(conserved[0], 0.05)
    velocity = conserved[1:4] / density
    internal = jnp.maximum(conserved[4] / density - 0.5 * lax.optimization_barrier(jnp.sum(velocity * velocity, axis=0)), 0.05)
    pressure = EOS_LINEAR * density * internal + EOS_QUAD * density * density
    return jnp.concatenate([density[None], velocity, pressure[None]], axis=0)

def fastest(conserved):
    prims = primitives(conserved)
    density = prims[0]
    sound = jnp.sqrt((EOS_QUAD * density * density + (1.0 + EOS_LINEAR) * prims[4]) / density)
    return jnp.max(jnp.abs(prims[1]) + jnp.abs(prims[2]) + jnp.abs(prims[3]) + 3.0 * sound)

def face_states(prims, sweep_axis):
    length = prims.shape[sweep_axis]
    inner = length - 8
    before = cut(prims, 0, length - 3, sweep_axis)
    centre_a = cut(prims, 1, length - 2, sweep_axis)
    centre_b = cut(prims, 2, length - 1, sweep_axis)
    after_b = cut(prims, 3, length, sweep_axis)
    faces = 7.0 / 12.0 * (centre_a + centre_b) - 1.0 / 12.0 * (before + after_b)
    faces = jnp.clip(faces, jnp.minimum(centre_a, centre_b), jnp.maximum(centre_a, centre_b))
    centre = cut(prims, 3, inner + 5, sweep_axis)
    left_edge = cut(faces, 1, inner + 3, sweep_axis)
    right_edge = cut(faces, 2, inner + 4, sweep_axis)
    pressure = prims[4:5]
    normal = prims[sweep_axis:sweep_axis + 1]
    near_diff = cut(pressure, 3, length - 1, sweep_axis) - cut(pressure, 1, length - 3, sweep_axis)
    far_diff = cut(pressure, 4, length, sweep_axis) - cut(pressure, 0, length - 4, sweep_axis)
    far_sum = cut(pressure, 4, length, sweep_axis) + cut(pressure, 0, length - 4, sweep_axis)
    steepness = jnp.abs(near_diff) / (jnp.abs(far_diff) + 0.1 * far_sum)
    squeeze = jnp.maximum(cut(normal, 1, length - 3, sweep_axis) - cut(normal, 3, length - 1, sweep_axis), 0.0)
    shock = jnp.clip((steepness - 0.75) * 4.0, 0.0, 1.0) * squeeze / (squeeze + 0.2)
    widest = jnp.maximum(jnp.maximum(cut(shock, 0, inner + 2, sweep_axis), cut(shock, 1, inner + 3, sweep_axis)), cut(shock, 2, inner + 4, sweep_axis))
    flatten = 1.0 - widest
    down_part = minmod(centre - left_edge, 2.0 * (right_edge - centre))
    up_part = minmod(right_edge - centre, 2.0 * (centre - left_edge))
    lower_val = centre - flatten * down_part
    upper_val = centre + flatten * up_part
    return (cut(upper_val, 0, inner + 1, sweep_axis), cut(lower_val, 1, inner + 2, sweep_axis))

def wave_side(prims):
    density = prims[0]
    pressure = prims[4]
    internal = jnp.maximum((pressure - EOS_QUAD * density * density) / (EOS_LINEAR * density), 0.05)
    impedance = jnp.sqrt(density * (EOS_QUAD * density * density + (1.0 + EOS_LINEAR) * pressure))
    gamma_eff = 1.0 + EOS_LINEAR + EOS_QUAD * density * density / pressure
    growth = (gamma_eff + 1.0) / (2.0 * gamma_eff)
    return (density, pressure, internal, impedance, growth)

def riemann(left_state, right_state, sweep_axis):
    dens_l, pres_l, int_l, imp_l, grow_l = wave_side(left_state)
    dens_r, pres_r, int_r, imp_r, grow_r = wave_side(right_state)
    vel_l = left_state[sweep_axis]
    vel_r = right_state[sweep_axis]
    floor_p = 0.1 * jnp.minimum(pres_l, pres_r)
    p_star = (imp_r * pres_l + imp_l * pres_r + imp_l * imp_r * (vel_l - vel_r)) / (imp_l + imp_r)
    p_star = jnp.maximum(p_star, floor_p)

    def speeds(guess):
        wave_l = imp_l * jnp.sqrt(1.0 + grow_l * (guess / pres_l - 1.0))
        wave_r = imp_r * jnp.sqrt(1.0 + grow_r * (guess / pres_r - 1.0))
        return (wave_l, wave_r)
    for sweep_turn in range(RIEMANN_ITERS):
        wave_l, wave_r = speeds(p_star)
        star_l = vel_l - (p_star - pres_l) / wave_l
        star_r = vel_r + (p_star - pres_r) / wave_r
        slope_l = 2.0 * wave_l ** 3 / (wave_l * wave_l + imp_l * imp_l)
        slope_r = 2.0 * wave_r ** 3 / (wave_r * wave_r + imp_r * imp_r)
        p_star = jnp.maximum(p_star - slope_l * slope_r * (star_r - star_l) / (slope_l + slope_r), floor_p)
    wave_l, wave_r = speeds(p_star)
    star_l = vel_l - (p_star - pres_l) / wave_l
    star_r = vel_r + (p_star - pres_r) / wave_r
    u_star = (wave_l * star_l + wave_r * star_r) / (wave_l + wave_r)
    vol_l = 1.0 / dens_l - (p_star - pres_l) / (wave_l * wave_l)
    vol_r = 1.0 / dens_r - (p_star - pres_r) / (wave_r * wave_r)
    inner_l = jnp.maximum(int_l + 0.5 * (p_star + pres_l) * (1.0 / dens_l - vol_l), 0.1 * int_l)
    inner_r = jnp.maximum(int_r + 0.5 * (p_star + pres_r) * (1.0 / dens_r - vol_r), 0.1 * int_r)
    upwind = u_star >= 0.0
    dens_star = jnp.where(upwind, 1.0 / vol_l, 1.0 / vol_r)
    inner_star = jnp.where(upwind, inner_l, inner_r)
    mass = dens_star * u_star
    kinetic = u_star * u_star
    momenta = []
    for component in range(1, 4):
        if component == sweep_axis:
            momenta.append(mass * u_star + p_star)
        else:
            carried = jnp.where(upwind, left_state[component], right_state[component])
            kinetic = kinetic + carried * carried
            momenta.append(mass * carried)
    energy = u_star * (dens_star * (inner_star + 0.5 * kinetic) + p_star)
    return jnp.stack([mass] + momenta + [energy], axis=0)

def rate(conserved, low_x, high_x, low_y, high_y, ratio):
    extended_x = jnp.concatenate([low_x, conserved, high_x], axis=1)
    extended_y = jnp.concatenate([low_y, conserved, high_y], axis=2)
    extended_z = jnp.concatenate([conserved[..., -GHOST:], conserved, conserved[..., :GHOST]], axis=3)
    tendency = jnp.zeros_like(conserved)
    for sweep_axis, extended in ((1, extended_x), (2, extended_y), (3, extended_z)):
        left_state, right_state = face_states(primitives(extended), sweep_axis)
        fluxes = riemann(left_state, right_state, sweep_axis)
        inner = conserved.shape[sweep_axis]
        tendency = tendency - ratio * (cut(fluxes, 1, inner + 1, sweep_axis) - cut(fluxes, 0, inner, sweep_axis))
    return tendency

def gather_ghosts(box_data, neighbours):
    lower = neighbours[:, 0]
    upper = neighbours[:, 1]
    beside = neighbours[:, 2]
    from_lower = jnp.take(box_data[:, :, -GHOST:], jnp.maximum(lower, 0), axis=0)
    from_upper = jnp.take(box_data[:, :, :GHOST], jnp.maximum(upper, 0), axis=0)
    edge_low = jnp.broadcast_to(box_data[:, :, :1], from_lower.shape)
    edge_high = jnp.broadcast_to(box_data[:, :, -1:], from_upper.shape)
    low_x = jnp.where((lower < 0)[:, None, None, None, None], edge_low, from_lower)
    high_x = jnp.where((upper < 0)[:, None, None, None, None], edge_high, from_upper)
    low_y = jnp.take(box_data[:, :, :, -GHOST:], beside, axis=0)
    high_y = jnp.take(box_data[:, :, :, :GHOST], beside, axis=0)
    return (low_x, high_x, low_y, high_y)

def apply_rate(box_data, neighbours, ratio):
    low_x, high_x, low_y, high_y = gather_ghosts(box_data, neighbours)

    def unpack_rate(bundle):
        return rate(bundle[0], bundle[1], bundle[2], bundle[3], bundle[4], ratio)
    return lax.map(unpack_rate, (box_data, low_x, high_x, low_y, high_y))

def reference(cell_state, swap_slots, neighbours):
    owners_count = NBOX // SLOTS
    box_shape = (FIELDS, BXC, BYC, BZC)
    shaped = cell_state.reshape((owners_count, SLOTS) + box_shape)
    owners = jnp.arange(owners_count, dtype=jnp.int32)
    outgoing = shaped[owners, swap_slots]
    incoming = outgoing[jnp.bitwise_xor(owners, owners_count // 2)]
    chosen = jnp.arange(SLOTS, dtype=jnp.int32)[None, :] == swap_slots[:, None]
    box_data = jnp.where(chosen[:, :, None, None, None, None], incoming[:, None], shaped).reshape((NBOX,) + box_shape)
    ratio = COURANT / jnp.max(lax.map(fastest, box_data))
    first = box_data + apply_rate(box_data, neighbours, ratio)
    result = 0.5 * (box_data + first + apply_rate(first, neighbours, ratio))
    return result.reshape(cell_state.shape)
```

```python
import functools

import jax
import jax.numpy as jnp
from jax import lax
from jax.experimental import pallas as pl
from jax.experimental.pallas import tpu as pltpu
from jax.sharding import PartitionSpec as P

BZC = 32
GHOST = 4
RIEMANN_ITERS = 3
COURANT = 0.4


def rcp(x):
    return pl.reciprocal(x, approx=True)


def primitives(u):
    density = jnp.maximum(u[0], 0.05)
    inv = 1.0 / density
    v1, v2, v3 = u[1] * inv, u[2] * inv, u[3] * inv
    internal = jnp.maximum(u[4] * inv - 0.5 * (v1 * v1 + v2 * v2 + v3 * v3), 0.05)
    pressure = density * (0.4 * internal + 0.1 * density)
    return density, v1, v2, v3, pressure


def signal_speed(q):
    sound = jnp.sqrt(0.1 * q[0] + 1.4 * q[4] / q[0])
    return jnp.abs(q[1]) + jnp.abs(q[2]) + jnp.abs(q[3]) + 3.0 * sound


def clip_to(x, span):
    return jnp.minimum(jnp.maximum(x, jnp.minimum(span, 0.0)), jnp.maximum(span, 0.0))


def face_offset(d_low, d, d_high):
    return clip_to(0.5 * d + (d_low - d_high) * (1.0 / 12.0), d)


def shock(near, far, far_sum, squeeze):
    steep = jnp.abs(near) * rcp(jnp.abs(far) + 0.1 * far_sum)
    squeeze = jnp.maximum(squeeze, 0.0)
    return jnp.clip(4.0 * steep - 3.0, 0.0, 1.0) * squeeze * rcp(squeeze + 0.2)


def edges(q, a, b, flat):
    lower = q - flat * clip_to(b + b, a)
    upper = q + flat * clip_to(a + a, b)
    return lower, upper


def wave_side(r, p):
    t = 0.1 * r * r
    c2 = r * (t + 1.4 * p)
    slope = 0.5 * r * (2.4 + t * rcp(p))
    return c2, slope, c2 - slope * p


def riemann(left, right, axis):
    r_l, u_l, p_l = left[0], left[axis], left[4]
    r_r, u_r, p_r = right[0], right[axis], right[4]
    c2_l, b_l, a_l = wave_side(r_l, p_l)
    c2_r, b_r, a_r = wave_side(r_r, p_r)
    c_l = c2_l * lax.rsqrt(c2_l)
    c_r = c2_r * lax.rsqrt(c2_r)
    floor_p = 0.1 * jnp.minimum(p_l, p_r)
    guess = (c_r * p_l + c_l * p_r + c_l * c_r * (u_l - u_r)) * rcp(c_l + c_r)
    guess = jnp.maximum(guess, floor_p)
    for _ in range(RIEMANN_ITERS):
        i_l = lax.rsqrt(a_l + b_l * guess)
        i_r = lax.rsqrt(a_r + b_r * guess)
        star_l = u_l - (guess - p_l) * i_l
        star_r = u_r + (guess - p_r) * i_r
        y_l = i_l + i_l * (c2_l * (i_l * i_l))
        y_r = i_r + i_r * (c2_r * (i_r * i_r))
        guess = jnp.maximum(guess - 2.0 * (star_r - star_l) * rcp(y_l + y_r), floor_p)
    w2_l = a_l + b_l * guess
    w2_r = a_r + b_r * guess
    w_l = w2_l * lax.rsqrt(w2_l)
    w_r = w2_r * lax.rsqrt(w2_r)
    u = (w_l * u_l + w_r * u_r + (p_l - p_r)) * rcp(w_l + w_r)
    upwind = u >= 0.0
    pick = lambda x, y: jnp.where(upwind, x, y)
    r, p, w2 = pick(r_l, r_r), pick(p_l, p_r), pick(w2_l, w2_r)
    inv_r = rcp(r)
    internal = jnp.maximum(2.5 * p * inv_r - 0.25 * r, 0.05)
    drop = (guess - p) * rcp(w2)
    inner = jnp.maximum(internal + 0.5 * (guess + p) * drop, 0.1 * internal)
    mass = u * rcp(inv_r - drop)
    kinetic = u * u
    momenta = []
    for component in (1, 2, 3):
        if component == axis:
            momenta.append(mass * u + guess)
        else:
            carried = pick(left[component], right[component])
            kinetic = kinetic + carried * carried
            momenta.append(mass * carried)
    return [mass] + momenta + [mass * (inner + 0.5 * kinetic) + u * guess]


def z_shift(x, n):
    z = lax.broadcasted_iota(jnp.int32, x.shape, x.ndim - 1) % BZC
    inside = pltpu.roll(x, (-n) % 128, x.ndim - 1)
    around = pltpu.roll(x, ((BZC if n > 0 else -BZC) - n) % 128, x.ndim - 1)
    keep = z < BZC - n if n > 0 else z >= -n
    return jnp.where(keep, inside, around)


def y_shift(x, n):
    lane = lax.broadcasted_iota(jnp.int32, x.shape, 2)
    row = lax.broadcasted_iota(jnp.int32, x.shape, 1)
    turned = pltpu.roll(x, (-n * BZC) % 128, 2)
    moved = pltpu.roll(turned, 7 if n > 0 else 1, 1)
    other = jnp.concatenate([moved[1:], moved[:1]], axis=0)
    carry = jnp.where(row == (7 if n > 0 else 0), other, moved)
    keep = lane < 128 - n * BZC if n > 0 else lane >= -n * BZC
    return jnp.where(keep, turned, carry)


def plane_sweep(q, shift, axis):
    d = [shift(x, 1) - x for x in q]
    d_low = [shift(x, -1) for x in d]
    d_high = [shift(x, 1) for x in d]
    b = [face_offset(l, m, h) for l, m, h in zip(d_low, d, d_high)]
    a = [shift(m - x, -1) for m, x in zip(d, b)]
    p_high = q[4] + (d[4] + d_high[4])
    p_low = shift(q[4], -2)
    chi = shock(d[4] + d_low[4], p_high - p_low, p_high + p_low, -(d[axis] + d_low[axis]))
    flat = 1.0 - jnp.maximum(jnp.maximum(shift(chi, -1), chi), shift(chi, 1))
    pairs = [edges(*x, flat) for x in zip(q, a, b)]
    flux = riemann([shift(x[1], -1) for x in pairs], [x[0] for x in pairs], axis)
    return [shift(x, 1) - x for x in flux]


def rate_kernel(last, ratio_ref, u_ref, base_ref, out_ref, q_ref, t_ref, a_ref, chi_ref, up_ref, flux_ref):
    depth = out_ref.shape[2]
    ratio = ratio_ref[0]

    @pl.loop(0, depth + 2 * GHOST)
    def _(e):
        q = primitives([u_ref[:, f, e] for f in range(5)])
        for f in range(5):
            q_ref[f, e] = q[f]

    @pl.loop(0, depth)
    def _(x):
        q = [q_ref[f, x + GHOST] for f in range(5)]
        dz = plane_sweep(q, z_shift, 3)
        dy = plane_sweep(q, y_shift, 2)
        for f in range(5):
            t_ref[f, x] = dz[f] + dy[f]

    def chi_at(e):
        low, high = q_ref[4, e - 2], q_ref[4, e + 2]
        return shock(
            q_ref[4, e + 1] - q_ref[4, e - 1], high - low, high + low, q_ref[1, e - 1] - q_ref[1, e + 1]
        )

    def cell(e):
        chi_next = chi_at(e + 1)
        flat = 1.0 - jnp.maximum(jnp.maximum(chi_ref[0], chi_ref[1]), chi_next)
        chi_ref[0] = chi_ref[1]
        chi_ref[1] = chi_next
        lower, upper = [], []
        for f in range(5):
            q = [q_ref[f, e + k] for k in (-1, 0, 1, 2)]
            d = q[2] - q[1]
            b = face_offset(q[1] - q[0], d, q[3] - q[2])
            low, high = edges(q[1], a_ref[f], b, flat)
            a_ref[f] = d - b
            lower.append(low)
            upper.append(high)
        return lower, upper

    for f in range(5):
        q = [q_ref[f, k] for k in (1, 2, 3, 4)]
        d = q[2] - q[1]
        a_ref[f] = d - face_offset(q[1] - q[0], d, q[3] - q[2])
    chi_ref[0] = chi_at(2)
    chi_ref[1] = chi_at(3)
    _, upper = cell(3)
    for f in range(5):
        up_ref[f] = upper[f]

    def face(e):
        lower, upper = cell(e)
        flux = riemann([up_ref[f] for f in range(5)], lower, 1)
        for f in range(5):
            up_ref[f] = upper[f]
        return flux

    flux = face(GHOST)
    for f in range(5):
        flux_ref[f] = flux[f]

    @pl.loop(0, depth)
    def _(x):
        flux = face(x + GHOST + 1)
        for f in range(5):
            u = u_ref[:, f, x + GHOST]
            new = u - ratio * (flux[f] - flux_ref[f] + t_ref[f, x])
            if last:
                new = 0.5 * (base_ref[:, f, x] + new)
            out_ref[:, f, x] = new
            flux_ref[f] = flux[f]


def rate_step(last, ratio, extended, base):
    slots, fields, depth = extended.shape[0], extended.shape[1], extended.shape[2] - 2 * GHOST
    tile = (slots, 8, 128)
    vmem = pl.BlockSpec(memory_space=pltpu.VMEM)
    return pl.pallas_call(
        functools.partial(rate_kernel, last),
        out_shape=jax.ShapeDtypeStruct((slots, fields, depth, 8, 128), jnp.float32),
        in_specs=[pl.BlockSpec(memory_space=pltpu.SMEM), vmem, vmem],
        out_specs=vmem,
        scratch_shapes=[
            pltpu.VMEM((fields, depth + 2 * GHOST) + tile, jnp.float32),
            pltpu.VMEM((fields, depth) + tile, jnp.float32),
            pltpu.VMEM((fields,) + tile, jnp.float32),
            pltpu.VMEM((2,) + tile, jnp.float32),
            pltpu.VMEM((fields,) + tile, jnp.float32),
            pltpu.VMEM((fields,) + tile, jnp.float32),
        ],
        compiler_params=pltpu.CompilerParams(vmem_limit_bytes=40 * 2**20),
    )(ratio, extended, base)


def extend(box_data, neighbours, own_start):
    slots = box_data.shape[0]
    count = lax.axis_size("box")
    below = lax.ppermute(box_data[:, :, -GHOST:], "box", [(i, i + 1) for i in range(count - 1)])
    above = lax.ppermute(box_data[:, :, :GHOST], "box", [(i + 1, i) for i in range(count - 1)])
    lower, upper = neighbours[:, 0], neighbours[:, 1]
    from_lower = jnp.take(below, jnp.clip(lower - own_start + slots, 0, slots - 1), axis=0)
    from_upper = jnp.take(above, jnp.clip(upper - own_start - slots, 0, slots - 1), axis=0)
    end = lambda x: (x < 0)[:, None, None, None, None]
    low = jnp.where(end(lower), box_data[:, :, :1], from_lower)
    high = jnp.where(end(upper), box_data[:, :, -1:], from_upper)
    return jnp.concatenate([low, box_data, high], axis=2)


def body(cell_state, swap_slots, neighbours):
    slots, fields, depth, _ = cell_state.shape
    cells = cell_state.reshape(slots, fields, depth, 8, 128)
    chosen_slot = swap_slots[0]
    count = lax.axis_size("box")
    outgoing = lax.dynamic_index_in_dim(cells, chosen_slot, 0, keepdims=False)
    incoming = lax.ppermute(outgoing, "box", [(i, i ^ (count // 2)) for i in range(count)])
    fast = jnp.max(signal_speed(primitives([cells[:, f] for f in range(fields)])))
    ratio = (COURANT / lax.pmax(fast, "box")).reshape(1)
    chosen = jnp.arange(slots, dtype=jnp.int32) == chosen_slot
    box_data = jnp.where(chosen[:, None, None, None, None], incoming[None], cells)
    own_start = lax.axis_index("box") * slots
    first = rate_step(False, ratio, extend(box_data, neighbours, own_start), box_data)
    new = rate_step(True, ratio, extend(first, neighbours, own_start), box_data)
    return new.reshape(cell_state.shape)


def solution(mesh):
    in_specs = (P("box", None, None, None), P("box"), P("box", None))
    out_specs = P("box", None, None, None)
    return jax.shard_map(body, mesh=mesh, in_specs=in_specs, out_specs=out_specs, check_vma=False)
```

```python
import functools

import jax
import jax.numpy as jnp
from jax import lax
from jax.experimental import pallas as pl
from jax.experimental.pallas import tpu as pltpu
from jax.sharding import PartitionSpec as P

BZC = 32
GHOST = 4
RIEMANN_ITERS = 3
COURANT = 0.4


def rcp(x):
    return pl.reciprocal(x, approx=True)


def primitives(u):
    density = jnp.maximum(u[0], 0.05)
    inv = 1.0 / density
    v1, v2, v3 = u[1] * inv, u[2] * inv, u[3] * inv
    internal = jnp.maximum(u[4] * inv - 0.5 * (v1 * v1 + v2 * v2 + v3 * v3), 0.05)
    pressure = density * (0.4 * internal + 0.1 * density)
    return density, v1, v2, v3, pressure


def signal_speed(q):
    sound = jnp.sqrt(0.1 * q[0] + 1.4 * q[4] / q[0])
    return jnp.abs(q[1]) + jnp.abs(q[2]) + jnp.abs(q[3]) + 3.0 * sound


def clip_to(x, span):
    return jnp.minimum(jnp.maximum(x, jnp.minimum(span, 0.0)), jnp.maximum(span, 0.0))


def face_offset(d_low, d, d_high):
    return clip_to(0.5 * d + (d_low - d_high) * (1.0 / 12.0), d)


def shock(near, far, far_sum, squeeze):
    steep = jnp.abs(near) * rcp(jnp.abs(far) + 0.1 * far_sum)
    squeeze = jnp.maximum(squeeze, 0.0)
    return jnp.clip(4.0 * steep - 3.0, 0.0, 1.0) * squeeze * rcp(squeeze + 0.2)


def edges(q, a, b, flat):
    lower = q - flat * clip_to(b + b, a)
    upper = q + flat * clip_to(a + a, b)
    return lower, upper


def wave_side(r, p):
    t = 0.1 * r * r
    c2 = r * (t + 1.4 * p)
    slope = 0.5 * r * (2.4 + t * rcp(p))
    return c2, slope, c2 - slope * p


def riemann(left, right, axis):
    r_l, u_l, p_l = left[0], left[axis], left[4]
    r_r, u_r, p_r = right[0], right[axis], right[4]
    c2_l, b_l, a_l = wave_side(r_l, p_l)
    c2_r, b_r, a_r = wave_side(r_r, p_r)
    c_l = c2_l * lax.rsqrt(c2_l)
    c_r = c2_r * lax.rsqrt(c2_r)
    floor_p = 0.1 * jnp.minimum(p_l, p_r)
    guess = (c_r * p_l + c_l * p_r + c_l * c_r * (u_l - u_r)) * rcp(c_l + c_r)
    guess = jnp.maximum(guess, floor_p)
    for _ in range(RIEMANN_ITERS):
        i_l = lax.rsqrt(a_l + b_l * guess)
        i_r = lax.rsqrt(a_r + b_r * guess)
        star_l = u_l - (guess - p_l) * i_l
        star_r = u_r + (guess - p_r) * i_r
        y_l = i_l + i_l * (c2_l * (i_l * i_l))
        y_r = i_r + i_r * (c2_r * (i_r * i_r))
        guess = jnp.maximum(guess - 2.0 * (star_r - star_l) * rcp(y_l + y_r), floor_p)
    w2_l = a_l + b_l * guess
    w2_r = a_r + b_r * guess
    w_l = w2_l * lax.rsqrt(w2_l)
    w_r = w2_r * lax.rsqrt(w2_r)
    u = (w_l * u_l + w_r * u_r + (p_l - p_r)) * rcp(w_l + w_r)
    upwind = u >= 0.0
    pick = lambda x, y: jnp.where(upwind, x, y)
    r, p, w2 = pick(r_l, r_r), pick(p_l, p_r), pick(w2_l, w2_r)
    inv_r = rcp(r)
    internal = jnp.maximum(2.5 * p * inv_r - 0.25 * r, 0.05)
    drop = (guess - p) * rcp(w2)
    inner = jnp.maximum(internal + 0.5 * (guess + p) * drop, 0.1 * internal)
    mass = u * rcp(inv_r - drop)
    kinetic = u * u
    momenta = []
    for component in (1, 2, 3):
        if component == axis:
            momenta.append(mass * u + guess)
        else:
            carried = pick(left[component], right[component])
            kinetic = kinetic + carried * carried
            momenta.append(mass * carried)
    return [mass] + momenta + [mass * (inner + 0.5 * kinetic) + u * guess]


def z_shift(x, n):
    z = lax.broadcasted_iota(jnp.int32, x.shape, x.ndim - 1) % BZC
    inside = pltpu.roll(x, (-n) % 128, x.ndim - 1)
    around = pltpu.roll(x, ((BZC if n > 0 else -BZC) - n) % 128, x.ndim - 1)
    keep = z < BZC - n if n > 0 else z >= -n
    return jnp.where(keep, inside, around)


def y_shift(x, n):
    lane = lax.broadcasted_iota(jnp.int32, x.shape, 2)
    row = lax.broadcasted_iota(jnp.int32, x.shape, 1)
    turned = pltpu.roll(x, (-n * BZC) % 128, 2)
    moved = pltpu.roll(turned, 7 if n > 0 else 1, 1)
    other = jnp.concatenate([moved[1:], moved[:1]], axis=0)
    carry = jnp.where(row == (7 if n > 0 else 0), other, moved)
    keep = lane < 128 - n * BZC if n > 0 else lane >= -n * BZC
    return jnp.where(keep, turned, carry)


def plane_sweep(q, shift, axis):
    d = [shift(x, 1) - x for x in q]
    d_low = [shift(x, -1) for x in d]
    d_high = [shift(x, 1) for x in d]
    b = [face_offset(l, m, h) for l, m, h in zip(d_low, d, d_high)]
    a = [shift(m - x, -1) for m, x in zip(d, b)]
    p_high = q[4] + (d[4] + d_high[4])
    p_low = shift(q[4], -2)
    chi = shock(d[4] + d_low[4], p_high - p_low, p_high + p_low, -(d[axis] + d_low[axis]))
    flat = 1.0 - jnp.maximum(jnp.maximum(shift(chi, -1), chi), shift(chi, 1))
    pairs = [edges(*x, flat) for x in zip(q, a, b)]
    flux = riemann([shift(x[1], -1) for x in pairs], [x[0] for x in pairs], axis)
    return [shift(x, 1) - x for x in flux]


def step_kernel(
    n, swap_ref, next_ref, cell_ref, out_ref,
    u_ref, first_ref, q_ref, t_ref, a_ref, chi_ref, up_ref, flux_ref, ratio_ref,
    sent_ref, came_ref, fast_ref, fast_in_ref, edge_ref, ghost_ref,
    swap_send, swap_recv, fast_send, fast_recv, edge_send, edge_recv,
):
    depth = out_ref.shape[2]
    chunks = depth // GHOST
    rounds = n.bit_length() - 1
    me = lax.axis_index("box")
    right, left = lax.rem(me + 1, n), lax.rem(me + n - 1, n)
    peers = [me + 2**k * (1 - 2 * lax.rem(lax.div(me, 2**k), 2)) for k in range(rounds)]
    sent_slot = swap_ref[0]
    kept_slot = 1 - sent_slot

    barrier = pltpu.get_barrier_semaphore()
    for peer in peers + [left, right]:
        pl.semaphore_signal(barrier, inc=1, device_id=(peer,), device_id_type=pl.DeviceIdType.MESH)
    pl.semaphore_wait(barrier, rounds + 2)

    def remote(src, dst, send, recv, peer):
        return pltpu.make_async_remote_copy(
            src_ref=src, dst_ref=dst, send_sem=send, recv_sem=recv,
            device_id=(peer,), device_id_type=pl.DeviceIdType.MESH,
        )

    def swap_copy(c):
        part = pl.ds(c * GHOST, GHOST)
        return remote(sent_ref.at[part], came_ref.at[part], swap_send.at[c], swap_recv.at[c], peers[-1])

    def fast_copy(k):
        return remote(fast_ref.at[k], fast_in_ref.at[k], fast_send.at[k], fast_recv.at[k], peers[k])

    def edge_copy(stage, side):
        i = 2 * stage + side
        return remote(edge_ref.at[i], ghost_ref.at[i], edge_send.at[i], edge_recv.at[i], (left, right)[side])

    @pl.loop(0, chunks)
    def _(j):
        c = lax.rem(j + chunks - 1, chunks)
        for k in range(GHOST):
            x = c * GHOST + k
            for f in range(5):
                sent_ref[x, f] = cell_ref[sent_slot, f, x]
        swap_copy(c).start()

    fast_ref[0] = jnp.zeros_like(fast_ref[0])

    @pl.loop(0, depth)
    def _(x):
        speed = signal_speed(primitives([cell_ref[:, f, x] for f in range(5)]))
        fast_ref[0] = jnp.maximum(fast_ref[0], jnp.maximum(speed[0], speed[1]))

    def kept(pair):
        x = 2 * pair
        u = [cell_ref[kept_slot, f, pl.ds(x, 2)] for f in range(5)]
        q = primitives(u)
        dz = plane_sweep(q, z_shift, 3)
        for f in range(5):
            for k in range(2):
                u_ref[f, x + k, 0] = u[f][k]
                q_ref[f, x + GHOST + k, 0] = q[f][k]
                t_ref[f, x + k, 0] = dz[f][k]

    pairs = depth // 2
    for k in range(rounds):
        fast_copy(k).start()
        pl.loop(pairs * k // rounds, pairs * (k + 1) // rounds)(kept)
        fast_copy(k).wait()
        fast_ref[k + 1] = jnp.maximum(fast_ref[k], fast_in_ref[k])
    ratio_ref[...] = jnp.zeros_like(ratio_ref) + COURANT / jnp.max(fast_ref[rounds], keepdims=True)

    def incoming(x):
        u = [came_ref[x, f] for f in range(5)]
        q = primitives(u)
        for f in range(5):
            u_ref[f, x, 1] = u[f]
            q_ref[f, x + GHOST, 1] = q[f]
        dz = plane_sweep([v[None] for v in q], z_shift, 3)
        dy = plane_sweep([q_ref[f, x + GHOST] for f in range(5)], y_shift, 2)
        for f in range(5):
            t_ref[f, x] = dy[f] + jnp.concatenate([t_ref[f, x, 0][None], dz[f]], axis=0)

    def both(x):
        q = primitives([first_ref[f, x] for f in range(5)])
        for f in range(5):
            q_ref[f, x + GHOST] = q[f]
        dz = plane_sweep(q, z_shift, 3)
        dy = plane_sweep(q, y_shift, 2)
        for f in range(5):
            t_ref[f, x] = dz[f] + dy[f]

    def by_slot(pair):
        return jnp.where(sent_slot == 0, pair[1], pair[0]), jnp.where(sent_slot == 0, pair[0], pair[1])

    def send_edge(stage, side, source_ref):
        @pl.loop(0, GHOST)
        def _(k):
            for f in range(5):
                zero, one = by_slot(source_ref[f, k + side * (depth - GHOST)])
                edge_ref[2 * stage + side, 0, k, f] = zero
                edge_ref[2 * stage + side, 1, k, f] = one

        edge_copy(stage, side).start()

    def take_ghosts(stage, side, source_ref):
        edge_copy(stage, 1 - side).wait()
        beside = [next_ref[slot, side] for slot in (kept_slot, sent_slot)]
        base = (left, right)[side] * 2
        own = side * (depth - 1)

        @pl.loop(0, GHOST)
        def _(k):
            u = []
            for f in range(5):
                mine = source_ref[f, own]
                parts = []
                for role in range(2):
                    zero, one = (ghost_ref[2 * stage + 1 - side, slot, k, f] for slot in range(2))
                    theirs = jnp.where(beside[role] == base, zero, one)
                    parts.append(jnp.where(beside[role] < 0, mine[role], theirs)[None])
                u.append(jnp.concatenate(parts, axis=0))
            q = primitives(u)
            for f in range(5):
                q_ref[f, k + side * (depth + GHOST)] = q[f]

    def chi_at(e):
        low, high = q_ref[4, e - 2], q_ref[4, e + 2]
        return shock(
            q_ref[4, e + 1] - q_ref[4, e - 1], high - low, high + low, q_ref[1, e - 1] - q_ref[1, e + 1]
        )

    def cell(e):
        chi_next = chi_at(e + 1)
        flat = 1.0 - jnp.maximum(jnp.maximum(chi_ref[0], chi_ref[1]), chi_next)
        chi_ref[0] = chi_ref[1]
        chi_ref[1] = chi_next
        lower, upper = [], []
        for f in range(5):
            q = [q_ref[f, e + k] for k in (-1, 0, 1, 2)]
            d = q[2] - q[1]
            b = face_offset(q[1] - q[0], d, q[3] - q[2])
            low, high = edges(q[1], a_ref[f], b, flat)
            a_ref[f] = d - b
            lower.append(low)
            upper.append(high)
        return lower, upper

    def face(e):
        lower, upper = cell(e)
        flux = riemann([up_ref[f] for f in range(5)], lower, 1)
        for f in range(5):
            up_ref[f] = upper[f]
        return flux

    def begin_x():
        for f in range(5):
            q = [q_ref[f, k] for k in (1, 2, 3, 4)]
            d = q[2] - q[1]
            a_ref[f] = d - face_offset(q[1] - q[0], d, q[3] - q[2])
        chi_ref[0] = chi_at(2)
        chi_ref[1] = chi_at(3)
        _, upper = cell(3)
        for f in range(5):
            up_ref[f] = upper[f]
        flux = face(GHOST)
        for f in range(5):
            flux_ref[f] = flux[f]

    def rate_x(x):
        flux = face(x + GHOST + 1)
        rate = []
        for f in range(5):
            rate.append(ratio_ref[...] * (flux[f] - flux_ref[f] + t_ref[f, x]))
            flux_ref[f] = flux[f]
        return rate

    def first_x(x):
        rate = rate_x(x)
        for f in range(5):
            first_ref[f, x] = u_ref[f, x] - rate[f]

    def last_x(x):
        rate = rate_x(x)
        for f in range(5):
            new = 0.5 * (u_ref[f, x] + (first_ref[f, x] - rate[f]))
            zero, one = by_slot(new)
            out_ref[0, f, x] = zero
            out_ref[1, f, x] = one

    swap_copy(chunks - 1).wait_recv()
    swap_copy(0).wait_recv()
    pl.loop(0, 2 * GHOST)(lambda j: incoming(lax.rem(j + depth - GHOST, depth)))
    send_edge(0, 1, u_ref)
    send_edge(0, 0, u_ref)

    def middle(c):
        swap_copy(c).wait_recv()
        pl.loop(0, GHOST)(lambda k: incoming(c * GHOST + k))

    middle(1)
    take_ghosts(0, 0, u_ref)
    begin_x()
    pl.loop(0, GHOST)(first_x)

    @pl.loop(2, chunks - 1)
    def _(c):
        middle(c)
        pl.loop(0, GHOST)(lambda k: first_x(c * GHOST - GHOST + k))

    take_ghosts(0, 1, u_ref)
    pl.loop(depth - 2 * GHOST, depth)(first_x)
    send_edge(1, 0, first_ref)
    send_edge(1, 1, first_ref)
    pl.loop(0, depth)(both)
    take_ghosts(1, 0, first_ref)
    take_ghosts(1, 1, first_ref)
    begin_x()
    pl.loop(0, depth)(last_x)
    pl.loop(0, chunks)(lambda c: swap_copy(c).wait_send())


def body(cell_state, swap_slots, neighbours):
    slots, fields, depth, _ = cell_state.shape
    n = lax.axis_size("box")
    rounds = n.bit_length() - 1
    cells = cell_state.reshape(slots, fields, depth, 8, 128)
    vmem, smem = (pl.BlockSpec(memory_space=space) for space in (pltpu.VMEM, pltpu.SMEM))
    pair = (slots, 8, 128)
    tile = (8, 128)
    scratch = [
        (fields, depth) + pair,
        (fields, depth) + pair,
        (fields, depth + 2 * GHOST) + pair,
        (fields, depth) + pair,
        (fields,) + pair,
        (2,) + pair,
        (fields,) + pair,
        (fields,) + pair,
        tile,
        (depth, fields) + tile,
        (depth, fields) + tile,
        (rounds + 1,) + tile,
        (rounds,) + tile,
        (4, slots, GHOST, fields) + tile,
        (4, slots, GHOST, fields) + tile,
    ]
    counts = [depth // GHOST] * 2 + [rounds] * 2 + [4] * 2
    new = pl.pallas_call(
        functools.partial(step_kernel, n),
        out_shape=jax.ShapeDtypeStruct(cells.shape, jnp.float32),
        in_specs=[smem, smem, vmem],
        out_specs=vmem,
        scratch_shapes=[pltpu.VMEM(s, jnp.float32) for s in scratch]
        + [pltpu.SemaphoreType.DMA((k,)) for k in counts],
        compiler_params=pltpu.CompilerParams(
            vmem_limit_bytes=40 * 2**20, collective_id=0, has_side_effects=True
        ),
    )(swap_slots, neighbours, cells)
    return new.reshape(cell_state.shape)


def solution(mesh):
    in_specs = (P("box", None, None, None), P("box"), P("box", None))
    out_specs = P("box", None, None, None)
    return jax.shard_map(body, mesh=mesh, in_specs=in_specs, out_specs=out_specs, check_vma=False)
```

```python
import functools

import jax
import jax.numpy as jnp
from jax import lax
from jax.experimental import pallas as pl
from jax.experimental.pallas import tpu as pltpu
from jax.sharding import PartitionSpec as P

BZC = 32
GHOST = 4
RIEMANN_ITERS = 3
COURANT = 0.4
XSTEP = 2


def rcp(x):
    return pl.reciprocal(x, approx=True)


def primitives(u):
    density = jnp.maximum(u[0], 0.05)
    inv = 1.0 / density
    v1, v2, v3 = u[1] * inv, u[2] * inv, u[3] * inv
    internal = jnp.maximum(u[4] * inv - 0.5 * (v1 * v1 + v2 * v2 + v3 * v3), 0.05)
    pressure = density * (0.4 * internal + 0.1 * density)
    return density, v1, v2, v3, pressure


def signal_speed(q):
    sound = jnp.sqrt(0.1 * q[0] + 1.4 * q[4] / q[0])
    return jnp.abs(q[1]) + jnp.abs(q[2]) + jnp.abs(q[3]) + 3.0 * sound


def clip_to(x, span):
    return jnp.minimum(jnp.maximum(x, jnp.minimum(span, 0.0)), jnp.maximum(span, 0.0))


def face_offset(d_low, d, d_high):
    return clip_to(0.5 * d + (d_low - d_high) * (1.0 / 12.0), d)


def shock(near, far, far_sum, squeeze):
    steep = jnp.abs(near) * rcp(jnp.abs(far) + 0.1 * far_sum)
    squeeze = jnp.maximum(squeeze, 0.0)
    return jnp.clip(4.0 * steep - 3.0, 0.0, 1.0) * squeeze * rcp(squeeze + 0.2)


def edges(q, a, b, flat):
    lower = q - flat * clip_to(b + b, a)
    upper = q + flat * clip_to(a + a, b)
    return lower, upper


def wave_side(r, p):
    t = 0.1 * r * r
    c2 = r * (t + 1.4 * p)
    slope = 0.5 * r * (2.4 + t * rcp(p))
    return c2, slope, c2 - slope * p


def riemann(left, right, axis):
    r_l, u_l, p_l = left[0], left[axis], left[4]
    r_r, u_r, p_r = right[0], right[axis], right[4]
    c2_l, b_l, a_l = wave_side(r_l, p_l)
    c2_r, b_r, a_r = wave_side(r_r, p_r)
    c_l = c2_l * lax.rsqrt(c2_l)
    c_r = c2_r * lax.rsqrt(c2_r)
    floor_p = 0.1 * jnp.minimum(p_l, p_r)
    guess = (c_r * p_l + c_l * p_r + c_l * c_r * (u_l - u_r)) * rcp(c_l + c_r)
    guess = jnp.maximum(guess, floor_p)
    for _ in range(RIEMANN_ITERS):
        i_l = lax.rsqrt(a_l + b_l * guess)
        i_r = lax.rsqrt(a_r + b_r * guess)
        star_l = u_l - (guess - p_l) * i_l
        star_r = u_r + (guess - p_r) * i_r
        y_l = i_l + i_l * (c2_l * (i_l * i_l))
        y_r = i_r + i_r * (c2_r * (i_r * i_r))
        guess = jnp.maximum(guess - 2.0 * (star_r - star_l) * rcp(y_l + y_r), floor_p)
    w2_l = a_l + b_l * guess
    w2_r = a_r + b_r * guess
    w_l = w2_l * lax.rsqrt(w2_l)
    w_r = w2_r * lax.rsqrt(w2_r)
    u = (w_l * u_l + w_r * u_r + (p_l - p_r)) * rcp(w_l + w_r)
    upwind = u >= 0.0
    pick = lambda x, y: jnp.where(upwind, x, y)
    r, p, w2 = pick(r_l, r_r), pick(p_l, p_r), pick(w2_l, w2_r)
    inv_r = rcp(r)
    internal = jnp.maximum(2.5 * p * inv_r - 0.25 * r, 0.05)
    drop = (guess - p) * rcp(w2)
    inner = jnp.maximum(internal + 0.5 * (guess + p) * drop, 0.1 * internal)
    mass = u * rcp(inv_r - drop)
    kinetic = u * u
    momenta = []
    for component in (1, 2, 3):
        if component == axis:
            momenta.append(mass * u + guess)
        else:
            carried = pick(left[component], right[component])
            kinetic = kinetic + carried * carried
            momenta.append(mass * carried)
    return [mass] + momenta + [mass * (inner + 0.5 * kinetic) + u * guess]


def z_shift(x, n):
    z = lax.broadcasted_iota(jnp.int32, x.shape, x.ndim - 1) % BZC
    inside = pltpu.roll(x, (-n) % 128, x.ndim - 1)
    around = pltpu.roll(x, ((BZC if n > 0 else -BZC) - n) % 128, x.ndim - 1)
    keep = z < BZC - n if n > 0 else z >= -n
    return jnp.where(keep, inside, around)


def y_shift(x, n):
    lane = lax.broadcasted_iota(jnp.int32, x.shape, 2)
    row = lax.broadcasted_iota(jnp.int32, x.shape, 1)
    turned = pltpu.roll(x, (-n * BZC) % 128, 2)
    moved = pltpu.roll(turned, 7 if n > 0 else 1, 1)
    other = jnp.concatenate([moved[i ^ 1][None] for i in range(x.shape[0])], axis=0)
    carry = jnp.where(row == (7 if n > 0 else 0), other, moved)
    keep = lane < 128 - n * BZC if n > 0 else lane >= -n * BZC
    return jnp.where(keep, turned, carry)


def plane_sweep(q, shift, axis):
    d = [shift(x, 1) - x for x in q]
    d_low = [shift(x, -1) for x in d]
    d_high = [shift(x, 1) for x in d]
    b = [face_offset(l, m, h) for l, m, h in zip(d_low, d, d_high)]
    a = [shift(m - x, -1) for m, x in zip(d, b)]
    p_high = q[4] + (d[4] + d_high[4])
    p_low = shift(q[4], -2)
    chi = shock(d[4] + d_low[4], p_high - p_low, p_high + p_low, -(d[axis] + d_low[axis]))
    flat = 1.0 - jnp.maximum(jnp.maximum(shift(chi, -1), chi), shift(chi, 1))
    pairs = [edges(*x, flat) for x in zip(q, a, b)]
    flux = riemann([shift(x[1], -1) for x in pairs], [x[0] for x in pairs], axis)
    return [shift(x, 1) - x for x in flux]


def step_kernel(
    n, swap_ref, next_ref, cell_ref, out_ref,
    u_ref, first_ref, q_ref, t_ref, a_ref, chi_ref, up_ref, flux_ref, ratio_ref,
    sent_ref, came_ref, fast_ref, fast_in_ref, edge_ref, ghost_ref,
    swap_send, swap_recv, fast_send, fast_recv, edge_send, edge_recv,
):
    depth = out_ref.shape[2]
    chunks = depth // GHOST
    rounds = n.bit_length() - 1
    me = lax.axis_index("box")
    right, left = lax.rem(me + 1, n), lax.rem(me + n - 1, n)
    peers = [me + 2**k * (1 - 2 * lax.rem(lax.div(me, 2**k), 2)) for k in range(rounds)]
    sent_slot = swap_ref[0]
    kept_slot = 1 - sent_slot

    barrier = pltpu.get_barrier_semaphore()
    for peer in peers + [left, right]:
        pl.semaphore_signal(barrier, inc=1, device_id=(peer,), device_id_type=pl.DeviceIdType.MESH)
    pl.semaphore_wait(barrier, rounds + 2)

    def remote(src, dst, send, recv, peer):
        return pltpu.make_async_remote_copy(
            src_ref=src, dst_ref=dst, send_sem=send, recv_sem=recv,
            device_id=(peer,), device_id_type=pl.DeviceIdType.MESH,
        )

    def swap_copy(c):
        part = pl.ds(c * GHOST, GHOST)
        return remote(sent_ref.at[part], came_ref.at[part], swap_send.at[c], swap_recv.at[c], peers[-1])

    def fast_copy(k):
        return remote(fast_ref.at[k], fast_in_ref.at[k], fast_send.at[k], fast_recv.at[k], peers[k])

    def edge_copy(stage, side):
        i = 2 * stage + side
        return remote(edge_ref.at[i], ghost_ref.at[i], edge_send.at[i], edge_recv.at[i], (left, right)[side])

    @pl.loop(0, chunks)
    def _(j):
        c = lax.rem(j + chunks - 1, chunks)
        for k in range(GHOST):
            x = c * GHOST + k
            for f in range(5):
                sent_ref[x, f] = cell_ref[sent_slot, f, x]
        swap_copy(c).start()

    fast_ref[0] = jnp.zeros_like(fast_ref[0])

    @pl.loop(0, chunks)
    def _(c):
        speed = signal_speed(primitives([cell_ref[:, f, pl.ds(c * GHOST, GHOST)] for f in range(5)]))
        fast_ref[0] = jnp.maximum(fast_ref[0], jnp.max(speed, axis=(0, 1)))

    def kept(c):
        x = c * GHOST
        u = [cell_ref[kept_slot, f, pl.ds(x, GHOST)] for f in range(5)]
        q = primitives(u)
        dz = plane_sweep(q, z_shift, 3)
        for f in range(5):
            for k in range(GHOST):
                u_ref[f, x + k, 0] = u[f][k]
                q_ref[f, x + GHOST + k, 0] = q[f][k]
                t_ref[f, x + k, 0] = dz[f][k]

    for k in range(rounds):
        fast_copy(k).start()
        pl.loop(chunks * k // rounds, chunks * (k + 1) // rounds)(kept)
        fast_copy(k).wait()
        fast_ref[k + 1] = jnp.maximum(fast_ref[k], fast_in_ref[k])
    ratio_ref[...] = jnp.zeros_like(ratio_ref) + COURANT / jnp.max(fast_ref[rounds], keepdims=True)

    def planes(ref, f, x, m):
        return ref[f, pl.ds(x, m)].reshape(2 * m, 8, 128)

    def put(ref, f, x, m, value):
        ref[f, pl.ds(x, m)] = value.reshape(m, 2, 8, 128)

    def incoming(x):
        u = [came_ref[pl.ds(x, 2), f] for f in range(5)]
        q = primitives(u)
        for f in range(5):
            for k in range(2):
                u_ref[f, x + k, 1] = u[f][k]
                q_ref[f, x + GHOST + k, 1] = q[f][k]
        dz = plane_sweep(q, z_shift, 3)
        dy = plane_sweep([planes(q_ref, f, x + GHOST, 2) for f in range(5)], y_shift, 2)
        for f in range(5):
            along_z = [part[None] for k in range(2) for part in (t_ref[f, x + k, 0], dz[f][k])]
            put(t_ref, f, x, 2, dy[f] + jnp.concatenate(along_z, axis=0))

    def both(x):
        q = primitives([planes(first_ref, f, x, 2) for f in range(5)])
        for f in range(5):
            put(q_ref, f, x + GHOST, 2, q[f])
        dz = plane_sweep(q, z_shift, 3)
        dy = plane_sweep(q, y_shift, 2)
        for f in range(5):
            put(t_ref, f, x, 2, dz[f] + dy[f])

    def by_slot(pair):
        return jnp.where(sent_slot == 0, pair[1], pair[0]), jnp.where(sent_slot == 0, pair[0], pair[1])

    def send_edge(stage, side, source_ref):
        @pl.loop(0, GHOST)
        def _(k):
            for f in range(5):
                zero, one = by_slot(source_ref[f, k + side * (depth - GHOST)])
                edge_ref[2 * stage + side, 0, k, f] = zero
                edge_ref[2 * stage + side, 1, k, f] = one

        edge_copy(stage, side).start()

    def take_ghosts(stage, side, source_ref):
        edge_copy(stage, 1 - side).wait()
        beside = [next_ref[slot, side] for slot in (kept_slot, sent_slot)]
        base = (left, right)[side] * 2
        own = side * (depth - 1)

        @pl.loop(0, GHOST)
        def _(k):
            u = []
            for f in range(5):
                mine = source_ref[f, own]
                parts = []
                for role in range(2):
                    zero, one = (ghost_ref[2 * stage + 1 - side, slot, k, f] for slot in range(2))
                    theirs = jnp.where(beside[role] == base, zero, one)
                    parts.append(jnp.where(beside[role] < 0, mine[role], theirs)[None])
                u.append(jnp.concatenate(parts, axis=0))
            q = primitives(u)
            for f in range(5):
                q_ref[f, k + side * (depth + GHOST)] = q[f]

    def chi_at(e, m):
        p = [planes(q_ref, 4, e + k, m) for k in (-2, -1, 1, 2)]
        v = [planes(q_ref, 1, e + k, m) for k in (-1, 1)]
        return shock(p[2] - p[1], p[3] - p[0], p[3] + p[0], v[0] - v[1])

    def shifted(first, rest):
        return first if rest.shape[0] == 2 else jnp.concatenate([first, rest[:-2]], axis=0)

    def cell(e, m):
        chi = jnp.concatenate([chi_ref[0], chi_ref[1], chi_at(e + 1, m)], axis=0)
        flat = 1.0 - jnp.maximum(jnp.maximum(chi[:-4], chi[2:-2]), chi[4:])
        chi_ref[0] = chi[-4:-2]
        chi_ref[1] = chi[-2:]
        lower, upper = [], []
        for f in range(5):
            q = [planes(q_ref, f, e + k, m) for k in (-1, 0, 1, 2)]
            d = q[2] - q[1]
            b = face_offset(q[1] - q[0], d, q[3] - q[2])
            a = d - b
            low, high = edges(q[1], shifted(a_ref[f], a), b, flat)
            a_ref[f] = a[-2:]
            lower.append(low)
            upper.append(high)
        return lower, upper

    def face(e, m):
        lower, upper = cell(e, m)
        flux = riemann([shifted(up_ref[f], upper[f]) for f in range(5)], lower, 1)
        for f in range(5):
            up_ref[f] = upper[f][-2:]
        return flux

    def begin_x():
        for f in range(5):
            q = [q_ref[f, k] for k in (1, 2, 3, 4)]
            d = q[2] - q[1]
            a_ref[f] = d - face_offset(q[1] - q[0], d, q[3] - q[2])
        chi_ref[0] = chi_at(2, 1)
        chi_ref[1] = chi_at(3, 1)
        _, upper = cell(3, 1)
        for f in range(5):
            up_ref[f] = upper[f]
        flux = face(GHOST, 1)
        for f in range(5):
            flux_ref[f] = flux[f]

    def rate_x(x):
        flux = face(x + GHOST + 1, XSTEP)
        rate = []
        for f in range(5):
            change = flux[f] - shifted(flux_ref[f], flux[f]) + planes(t_ref, f, x, XSTEP)
            rate.append(ratio_ref[...] * change)
            flux_ref[f] = flux[f][-2:]
        return rate

    def first_x(x):
        rate = rate_x(x)
        for f in range(5):
            put(first_ref, f, x, XSTEP, planes(u_ref, f, x, XSTEP) - rate[f])

    def last_x(x):
        rate = rate_x(x)
        for f in range(5):
            new = 0.5 * (planes(u_ref, f, x, XSTEP) + (planes(first_ref, f, x, XSTEP) - rate[f]))
            for k in range(XSTEP):
                zero, one = by_slot(new[2 * k : 2 * k + 2])
                out_ref[0, f, x + k] = zero
                out_ref[1, f, x + k] = one

    swap_copy(chunks - 1).wait_recv()
    swap_copy(0).wait_recv()
    pl.loop(0, GHOST)(lambda j: incoming(lax.rem(2 * j + depth - GHOST, depth)))
    send_edge(0, 1, u_ref)
    send_edge(0, 0, u_ref)

    def middle(c):
        swap_copy(c).wait_recv()
        pl.loop(0, GHOST // 2)(lambda k: incoming(c * GHOST + 2 * k))

    middle(1)
    take_ghosts(0, 0, u_ref)
    begin_x()
    pl.loop(0, GHOST, step=XSTEP)(first_x)

    @pl.loop(2, chunks - 1)
    def _(c):
        middle(c)
        pl.loop(0, GHOST, step=XSTEP)(lambda k: first_x(c * GHOST - GHOST + k))

    take_ghosts(0, 1, u_ref)
    pl.loop(depth - 2 * GHOST, depth, step=XSTEP)(first_x)
    send_edge(1, 0, first_ref)
    send_edge(1, 1, first_ref)
    pl.loop(0, depth, step=2)(both)
    take_ghosts(1, 0, first_ref)
    take_ghosts(1, 1, first_ref)
    begin_x()
    pl.loop(0, depth, step=XSTEP)(last_x)
    pl.loop(0, chunks)(lambda c: swap_copy(c).wait_send())


def body(cell_state, swap_slots, neighbours):
    slots, fields, depth, _ = cell_state.shape
    n = lax.axis_size("box")
    rounds = n.bit_length() - 1
    cells = cell_state.reshape(slots, fields, depth, 8, 128)
    vmem, smem = (pl.BlockSpec(memory_space=space) for space in (pltpu.VMEM, pltpu.SMEM))
    pair = (slots, 8, 128)
    tile = (8, 128)
    scratch = [
        (fields, depth) + pair,
        (fields, depth) + pair,
        (fields, depth + 2 * GHOST) + pair,
        (fields, depth) + pair,
        (fields,) + pair,
        (2,) + pair,
        (fields,) + pair,
        (fields,) + pair,
        tile,
        (depth, fields) + tile,
        (depth, fields) + tile,
        (rounds + 1,) + tile,
        (rounds,) + tile,
        (4, slots, GHOST, fields) + tile,
        (4, slots, GHOST, fields) + tile,
    ]
    counts = [depth // GHOST] * 2 + [rounds] * 2 + [4] * 2
    new = pl.pallas_call(
        functools.partial(step_kernel, n),
        out_shape=jax.ShapeDtypeStruct(cells.shape, jnp.float32),
        in_specs=[smem, smem, vmem],
        out_specs=vmem,
        scratch_shapes=[pltpu.VMEM(s, jnp.float32) for s in scratch]
        + [pltpu.SemaphoreType.DMA((k,)) for k in counts],
        compiler_params=pltpu.CompilerParams(
            vmem_limit_bytes=40 * 2**20, collective_id=0, has_side_effects=True
        ),
    )(swap_slots, neighbours, cells)
    return new.reshape(cell_state.shape)


def solution(mesh):
    in_specs = (P("box", None, None, None), P("box"), P("box", None))
    out_specs = P("box", None, None, None)
    return jax.shard_map(body, mesh=mesh, in_specs=in_specs, out_specs=out_specs, check_vma=False)
```

```python
import functools

import jax
import jax.numpy as jnp
from jax import lax
from jax.experimental import pallas as pl
from jax.experimental.pallas import tpu as pltpu
from jax.sharding import PartitionSpec as P

BZC = 32
GHOST = 4
RIEMANN_ITERS = 3
COURANT = 0.4
XSTEP = 2
IN_FLIGHT = 3


def rcp(x):
    return pl.reciprocal(x, approx=True)


def primitives(u):
    density = jnp.maximum(u[0], 0.05)
    inv = 1.0 / density
    v1, v2, v3 = u[1] * inv, u[2] * inv, u[3] * inv
    internal = jnp.maximum(u[4] * inv - 0.5 * (v1 * v1 + v2 * v2 + v3 * v3), 0.05)
    pressure = density * (0.4 * internal + 0.1 * density)
    return density, v1, v2, v3, pressure


def signal_speed(q):
    sound = jnp.sqrt(0.1 * q[0] + 1.4 * q[4] / q[0])
    return jnp.abs(q[1]) + jnp.abs(q[2]) + jnp.abs(q[3]) + 3.0 * sound


def clip_to(x, span):
    return jnp.minimum(jnp.maximum(x, jnp.minimum(span, 0.0)), jnp.maximum(span, 0.0))


def face_offset(d_low, d, d_high):
    return clip_to(0.5 * d + (d_low - d_high) * (1.0 / 12.0), d)


def shock(near, far, far_sum, squeeze):
    steep = jnp.abs(near) * rcp(jnp.abs(far) + 0.1 * far_sum)
    squeeze = jnp.maximum(squeeze, 0.0)
    return jnp.clip(4.0 * steep - 3.0, 0.0, 1.0) * squeeze * rcp(squeeze + 0.2)


def edges(q, a, b, flat):
    lower = q - flat * clip_to(b + b, a)
    upper = q + flat * clip_to(a + a, b)
    return lower, upper


def wave_side(r, p):
    t = 0.1 * r * r
    c2 = r * (t + 1.4 * p)
    slope = 0.5 * r * (2.4 + t * rcp(p))
    return c2, slope, c2 - slope * p


def riemann(left, right, axis):
    r_l, u_l, p_l = left[0], left[axis], left[4]
    r_r, u_r, p_r = right[0], right[axis], right[4]
    c2_l, b_l, a_l = wave_side(r_l, p_l)
    c2_r, b_r, a_r = wave_side(r_r, p_r)
    c_l = c2_l * lax.rsqrt(c2_l)
    c_r = c2_r * lax.rsqrt(c2_r)
    floor_p = 0.1 * jnp.minimum(p_l, p_r)
    guess = (c_r * p_l + c_l * p_r + c_l * c_r * (u_l - u_r)) * rcp(c_l + c_r)
    guess = jnp.maximum(guess, floor_p)
    for _ in range(RIEMANN_ITERS):
        i_l = lax.rsqrt(a_l + b_l * guess)
        i_r = lax.rsqrt(a_r + b_r * guess)
        star_l = u_l - (guess - p_l) * i_l
        star_r = u_r + (guess - p_r) * i_r
        y_l = i_l + i_l * (c2_l * (i_l * i_l))
        y_r = i_r + i_r * (c2_r * (i_r * i_r))
        guess = jnp.maximum(guess - 2.0 * (star_r - star_l) * rcp(y_l + y_r), floor_p)
    w2_l = a_l + b_l * guess
    w2_r = a_r + b_r * guess
    w_l = w2_l * lax.rsqrt(w2_l)
    w_r = w2_r * lax.rsqrt(w2_r)
    u = (w_l * u_l + w_r * u_r + (p_l - p_r)) * rcp(w_l + w_r)
    upwind = u >= 0.0
    pick = lambda x, y: jnp.where(upwind, x, y)
    r, p, w2 = pick(r_l, r_r), pick(p_l, p_r), pick(w2_l, w2_r)
    inv_r = rcp(r)
    internal = jnp.maximum(2.5 * p * inv_r - 0.25 * r, 0.05)
    drop = (guess - p) * rcp(w2)
    inner = jnp.maximum(internal + 0.5 * (guess + p) * drop, 0.1 * internal)
    mass = u * rcp(inv_r - drop)
    kinetic = u * u
    momenta = []
    for component in (1, 2, 3):
        if component == axis:
            momenta.append(mass * u + guess)
        else:
            carried = pick(left[component], right[component])
            kinetic = kinetic + carried * carried
            momenta.append(mass * carried)
    return [mass] + momenta + [mass * (inner + 0.5 * kinetic) + u * guess]


def z_shift(x, n):
    z = lax.broadcasted_iota(jnp.int32, x.shape, x.ndim - 1) % BZC
    inside = pltpu.roll(x, (-n) % 128, x.ndim - 1)
    around = pltpu.roll(x, ((BZC if n > 0 else -BZC) - n) % 128, x.ndim - 1)
    keep = z < BZC - n if n > 0 else z >= -n
    return jnp.where(keep, inside, around)


def y_shift(x, n):
    lane = lax.broadcasted_iota(jnp.int32, x.shape, 2)
    row = lax.broadcasted_iota(jnp.int32, x.shape, 1)
    turned = pltpu.roll(x, (-n * BZC) % 128, 2)
    moved = pltpu.roll(turned, 7 if n > 0 else 1, 1)
    other = jnp.concatenate([moved[i ^ 1][None] for i in range(x.shape[0])], axis=0)
    carry = jnp.where(row == (7 if n > 0 else 0), other, moved)
    keep = lane < 128 - n * BZC if n > 0 else lane >= -n * BZC
    return jnp.where(keep, turned, carry)


def plane_sweep(q, shift, axis):
    d = [shift(x, 1) - x for x in q]
    d_low = [shift(x, -1) for x in d]
    d_high = [shift(x, 1) for x in d]
    b = [face_offset(l, m, h) for l, m, h in zip(d_low, d, d_high)]
    a = [shift(m - x, -1) for m, x in zip(d, b)]
    p_high = q[4] + (d[4] + d_high[4])
    p_low = shift(q[4], -2)
    chi = shock(d[4] + d_low[4], p_high - p_low, p_high + p_low, -(d[axis] + d_low[axis]))
    flat = 1.0 - jnp.maximum(jnp.maximum(shift(chi, -1), chi), shift(chi, 1))
    pairs = [edges(*x, flat) for x in zip(q, a, b)]
    flux = riemann([shift(x[1], -1) for x in pairs], [x[0] for x in pairs], axis)
    return [shift(x, 1) - x for x in flux]


def step_kernel(
    n, swap_ref, next_ref, cell_ref, out_ref,
    u_ref, first_ref, q_ref, t_ref, a_ref, chi_ref, up_ref, flux_ref, ratio_ref,
    sent_ref, came_ref, fast_ref, fast_in_ref, edge_ref, ghost_ref,
    swap_send, swap_recv, fast_send, fast_recv, edge_send, edge_recv,
):
    depth = out_ref.shape[2]
    chunks = depth // GHOST
    rounds = n.bit_length() - 1
    me = lax.axis_index("box")
    right, left = lax.rem(me + 1, n), lax.rem(me + n - 1, n)
    peers = [me + 2**k * (1 - 2 * lax.rem(lax.div(me, 2**k), 2)) for k in range(rounds)]
    sent_slot = swap_ref[0]
    kept_slot = 1 - sent_slot

    barrier = pltpu.get_barrier_semaphore()
    for peer in peers + [left, right]:
        pl.semaphore_signal(barrier, inc=1, device_id=(peer,), device_id_type=pl.DeviceIdType.MESH)
    pl.semaphore_wait(barrier, rounds + 2)

    def remote(src, dst, send, recv, peer):
        return pltpu.make_async_remote_copy(
            src_ref=src, dst_ref=dst, send_sem=send, recv_sem=recv,
            device_id=(peer,), device_id_type=pl.DeviceIdType.MESH,
        )

    def swap_copy(c):
        part = pl.ds(c * GHOST, GHOST)
        return remote(sent_ref.at[part], came_ref.at[part], swap_send.at[c], swap_recv.at[c], peers[-1])

    def fast_copy(k):
        return remote(fast_ref.at[k], fast_in_ref.at[k], fast_send.at[k], fast_recv.at[k], peers[k])

    def edge_copy(stage, side):
        i = 2 * stage + side
        return remote(edge_ref.at[i], ghost_ref.at[i], edge_send.at[i], edge_recv.at[i], (left, right)[side])

    def chunk(j):
        return lax.rem(j + chunks - 1, chunks)

    def launch(j):
        c = chunk(j)
        for k in range(GHOST):
            x = c * GHOST + k
            for f in range(5):
                sent_ref[x, f] = cell_ref[sent_slot, f, x]
        swap_copy(c).start()

    def arrive(j):
        swap_copy(chunk(j)).wait()

        @pl.when(j + IN_FLIGHT < chunks)
        def _():
            launch(j + IN_FLIGHT)

    pl.loop(0, IN_FLIGHT)(launch)
    fast_ref[0] = jnp.zeros_like(fast_ref[0])

    @pl.loop(0, chunks)
    def _(c):
        speed = signal_speed(primitives([cell_ref[:, f, pl.ds(c * GHOST, GHOST)] for f in range(5)]))
        fast_ref[0] = jnp.maximum(fast_ref[0], jnp.max(speed, axis=(0, 1)))

    def kept(c):
        x = c * GHOST
        u = [cell_ref[kept_slot, f, pl.ds(x, GHOST)] for f in range(5)]
        q = primitives(u)
        dz = plane_sweep(q, z_shift, 3)
        for f in range(5):
            for k in range(GHOST):
                u_ref[f, x + k, 0] = u[f][k]
                q_ref[f, x + GHOST + k, 0] = q[f][k]
                t_ref[f, x + k, 0] = dz[f][k]

    for k in range(rounds):
        fast_copy(k).start()
        pl.loop(chunks * k // rounds, chunks * (k + 1) // rounds)(kept)
        fast_copy(k).wait()
        fast_ref[k + 1] = jnp.maximum(fast_ref[k], fast_in_ref[k])
    ratio_ref[...] = jnp.zeros_like(ratio_ref) + COURANT / jnp.max(fast_ref[rounds], keepdims=True)

    def planes(ref, f, x, m):
        return ref[f, pl.ds(x, m)].reshape(2 * m, 8, 128)

    def put(ref, f, x, m, value):
        ref[f, pl.ds(x, m)] = value.reshape(m, 2, 8, 128)

    def incoming(x):
        u = [came_ref[pl.ds(x, 2), f] for f in range(5)]
        q = primitives(u)
        for f in range(5):
            for k in range(2):
                u_ref[f, x + k, 1] = u[f][k]
                q_ref[f, x + GHOST + k, 1] = q[f][k]
        dz = plane_sweep(q, z_shift, 3)
        dy = plane_sweep([planes(q_ref, f, x + GHOST, 2) for f in range(5)], y_shift, 2)
        for f in range(5):
            along_z = [part[None] for k in range(2) for part in (t_ref[f, x + k, 0], dz[f][k])]
            put(t_ref, f, x, 2, dy[f] + jnp.concatenate(along_z, axis=0))

    def both(x):
        q = primitives([planes(first_ref, f, x, 2) for f in range(5)])
        for f in range(5):
            put(q_ref, f, x + GHOST, 2, q[f])
        dz = plane_sweep(q, z_shift, 3)
        dy = plane_sweep(q, y_shift, 2)
        for f in range(5):
            put(t_ref, f, x, 2, dz[f] + dy[f])

    def by_slot(pair):
        return jnp.where(sent_slot == 0, pair[1], pair[0]), jnp.where(sent_slot == 0, pair[0], pair[1])

    def send_edge(stage, side, source_ref):
        @pl.loop(0, GHOST)
        def _(k):
            for f in range(5):
                zero, one = by_slot(source_ref[f, k + side * (depth - GHOST)])
                edge_ref[2 * stage + side, 0, k, f] = zero
                edge_ref[2 * stage + side, 1, k, f] = one

        edge_copy(stage, side).start()

    def take_ghosts(stage, side, source_ref):
        edge_copy(stage, 1 - side).wait()
        beside = [next_ref[slot, side] for slot in (kept_slot, sent_slot)]
        base = (left, right)[side] * 2
        own = side * (depth - 1)

        @pl.loop(0, GHOST)
        def _(k):
            u = []
            for f in range(5):
                mine = source_ref[f, own]
                parts = []
                for role in range(2):
                    zero, one = (ghost_ref[2 * stage + 1 - side, slot, k, f] for slot in range(2))
                    theirs = jnp.where(beside[role] == base, zero, one)
                    parts.append(jnp.where(beside[role] < 0, mine[role], theirs)[None])
                u.append(jnp.concatenate(parts, axis=0))
            q = primitives(u)
            for f in range(5):
                q_ref[f, k + side * (depth + GHOST)] = q[f]

    def chi_at(e, m):
        p = [planes(q_ref, 4, e + k, m) for k in (-2, -1, 1, 2)]
        v = [planes(q_ref, 1, e + k, m) for k in (-1, 1)]
        return shock(p[2] - p[1], p[3] - p[0], p[3] + p[0], v[0] - v[1])

    def shifted(first, rest):
        return first if rest.shape[0] == 2 else jnp.concatenate([first, rest[:-2]], axis=0)

    def cell(e, m):
        chi = jnp.concatenate([chi_ref[0], chi_ref[1], chi_at(e + 1, m)], axis=0)
        flat = 1.0 - jnp.maximum(jnp.maximum(chi[:-4], chi[2:-2]), chi[4:])
        chi_ref[0] = chi[-4:-2]
        chi_ref[1] = chi[-2:]
        lower, upper = [], []
        for f in range(5):
            q = [planes(q_ref, f, e + k, m) for k in (-1, 0, 1, 2)]
            d = q[2] - q[1]
            b = face_offset(q[1] - q[0], d, q[3] - q[2])
            a = d - b
            low, high = edges(q[1], shifted(a_ref[f], a), b, flat)
            a_ref[f] = a[-2:]
            lower.append(low)
            upper.append(high)
        return lower, upper

    def face(e, m):
        lower, upper = cell(e, m)
        flux = riemann([shifted(up_ref[f], upper[f]) for f in range(5)], lower, 1)
        for f in range(5):
            up_ref[f] = upper[f][-2:]
        return flux

    def begin_x():
        for f in range(5):
            q = [q_ref[f, k] for k in (1, 2, 3, 4)]
            d = q[2] - q[1]
            a_ref[f] = d - face_offset(q[1] - q[0], d, q[3] - q[2])
        chi_ref[0] = chi_at(2, 1)
        chi_ref[1] = chi_at(3, 1)
        _, upper = cell(3, 1)
        for f in range(5):
            up_ref[f] = upper[f]
        flux = face(GHOST, 1)
        for f in range(5):
            flux_ref[f] = flux[f]

    def rate_x(x):
        flux = face(x + GHOST + 1, XSTEP)
        rate = []
        for f in range(5):
            change = flux[f] - shifted(flux_ref[f], flux[f]) + planes(t_ref, f, x, XSTEP)
            rate.append(ratio_ref[...] * change)
            flux_ref[f] = flux[f][-2:]
        return rate

    def first_x(x):
        rate = rate_x(x)
        for f in range(5):
            put(first_ref, f, x, XSTEP, planes(u_ref, f, x, XSTEP) - rate[f])

    def last_x(x):
        rate = rate_x(x)
        for f in range(5):
            new = 0.5 * (planes(u_ref, f, x, XSTEP) + (planes(first_ref, f, x, XSTEP) - rate[f]))
            for k in range(XSTEP):
                zero, one = by_slot(new[2 * k : 2 * k + 2])
                out_ref[0, f, x + k] = zero
                out_ref[1, f, x + k] = one

    arrive(0)
    arrive(1)
    pl.loop(0, GHOST)(lambda j: incoming(lax.rem(2 * j + depth - GHOST, depth)))
    send_edge(0, 1, u_ref)
    send_edge(0, 0, u_ref)

    def middle(c):
        arrive(c + 1)
        pl.loop(0, GHOST // 2)(lambda k: incoming(c * GHOST + 2 * k))

    middle(1)
    take_ghosts(0, 0, u_ref)
    begin_x()
    pl.loop(0, GHOST, step=XSTEP)(first_x)

    @pl.loop(2, chunks - 1)
    def _(c):
        middle(c)
        pl.loop(0, GHOST, step=XSTEP)(lambda k: first_x(c * GHOST - GHOST + k))

    take_ghosts(0, 1, u_ref)
    pl.loop(depth - 2 * GHOST, depth, step=XSTEP)(first_x)
    send_edge(1, 0, first_ref)
    send_edge(1, 1, first_ref)
    pl.loop(0, depth, step=2)(both)
    take_ghosts(1, 0, first_ref)
    take_ghosts(1, 1, first_ref)
    begin_x()
    pl.loop(0, depth, step=XSTEP)(last_x)


def body(cell_state, swap_slots, neighbours):
    slots, fields, depth, _ = cell_state.shape
    n = lax.axis_size("box")
    rounds = n.bit_length() - 1
    cells = cell_state.reshape(slots, fields, depth, 8, 128)
    vmem, smem = (pl.BlockSpec(memory_space=space) for space in (pltpu.VMEM, pltpu.SMEM))
    pair = (slots, 8, 128)
    tile = (8, 128)
    scratch = [
        (fields, depth) + pair,
        (fields, depth) + pair,
        (fields, depth + 2 * GHOST) + pair,
        (fields, depth) + pair,
        (fields,) + pair,
        (2,) + pair,
        (fields,) + pair,
        (fields,) + pair,
        tile,
        (depth, fields) + tile,
        (depth, fields) + tile,
        (rounds + 1,) + tile,
        (rounds,) + tile,
        (4, slots, GHOST, fields) + tile,
        (4, slots, GHOST, fields) + tile,
    ]
    counts = [depth // GHOST] * 2 + [rounds] * 2 + [4] * 2
    new = pl.pallas_call(
        functools.partial(step_kernel, n),
        out_shape=jax.ShapeDtypeStruct(cells.shape, jnp.float32),
        in_specs=[smem, smem, vmem],
        out_specs=vmem,
        scratch_shapes=[pltpu.VMEM(s, jnp.float32) for s in scratch]
        + [pltpu.SemaphoreType.DMA((k,)) for k in counts],
        compiler_params=pltpu.CompilerParams(
            vmem_limit_bytes=40 * 2**20, collective_id=0, has_side_effects=True
        ),
    )(swap_slots, neighbours, cells)
    return new.reshape(cell_state.shape)


def solution(mesh):
    in_specs = (P("box", None, None, None), P("box"), P("box", None))
    out_specs = P("box", None, None, None)
    return jax.shard_map(body, mesh=mesh, in_specs=in_specs, out_specs=out_specs, check_vma=False)
```

```python
import functools

import jax
import jax.numpy as jnp
from jax import lax
from jax.experimental import pallas as pl
from jax.experimental.pallas import tpu as pltpu
from jax.sharding import PartitionSpec as P

BZC = 32
GHOST = 4
RIEMANN_ITERS = 3
COURANT = 0.4
XSTEP = 2
IN_FLIGHT = 3
LEAD = 8


def rcp(x):
    return pl.reciprocal(x, approx=True)


def primitives(u):
    density = jnp.maximum(u[0], 0.05)
    inv = 1.0 / density
    v1, v2, v3 = u[1] * inv, u[2] * inv, u[3] * inv
    internal = jnp.maximum(u[4] * inv - 0.5 * (v1 * v1 + v2 * v2 + v3 * v3), 0.05)
    pressure = density * (0.4 * internal + 0.1 * density)
    return density, v1, v2, v3, pressure


def signal_speed(q):
    sound = jnp.sqrt(0.1 * q[0] + 1.4 * q[4] / q[0])
    return jnp.abs(q[1]) + jnp.abs(q[2]) + jnp.abs(q[3]) + 3.0 * sound


def clip_to(x, span):
    return jnp.minimum(jnp.maximum(x, jnp.minimum(span, 0.0)), jnp.maximum(span, 0.0))


def face_offset(d_low, d, d_high):
    return clip_to(0.5 * d + (d_low - d_high) * (1.0 / 12.0), d)


def shock(near, far, far_sum, squeeze):
    steep = jnp.abs(near) * rcp(jnp.abs(far) + 0.1 * far_sum)
    squeeze = jnp.maximum(squeeze, 0.0)
    return jnp.clip(4.0 * steep - 3.0, 0.0, 1.0) * squeeze * rcp(squeeze + 0.2)


def edges(q, a, b, flat):
    lower = q - flat * clip_to(b + b, a)
    upper = q + flat * clip_to(a + a, b)
    return lower, upper


def wave_side(r, p):
    t = 0.1 * r * r
    c2 = r * (t + 1.4 * p)
    slope = 0.5 * r * (2.4 + t * rcp(p))
    return c2, slope, c2 - slope * p


def riemann(left, right, axis):
    r_l, u_l, p_l = left[0], left[axis], left[4]
    r_r, u_r, p_r = right[0], right[axis], right[4]
    c2_l, b_l, a_l = wave_side(r_l, p_l)
    c2_r, b_r, a_r = wave_side(r_r, p_r)
    c_l = c2_l * lax.rsqrt(c2_l)
    c_r = c2_r * lax.rsqrt(c2_r)
    floor_p = 0.1 * jnp.minimum(p_l, p_r)
    guess = (c_r * p_l + c_l * p_r + c_l * c_r * (u_l - u_r)) * rcp(c_l + c_r)
    guess = jnp.maximum(guess, floor_p)
    for _ in range(RIEMANN_ITERS):
        i_l = lax.rsqrt(a_l + b_l * guess)
        i_r = lax.rsqrt(a_r + b_r * guess)
        star_l = u_l - (guess - p_l) * i_l
        star_r = u_r + (guess - p_r) * i_r
        y_l = i_l + i_l * (c2_l * (i_l * i_l))
        y_r = i_r + i_r * (c2_r * (i_r * i_r))
        guess = jnp.maximum(guess - 2.0 * (star_r - star_l) * rcp(y_l + y_r), floor_p)
    w2_l = a_l + b_l * guess
    w2_r = a_r + b_r * guess
    w_l = w2_l * lax.rsqrt(w2_l)
    w_r = w2_r * lax.rsqrt(w2_r)
    u = (w_l * u_l + w_r * u_r + (p_l - p_r)) * rcp(w_l + w_r)
    upwind = u >= 0.0
    pick = lambda x, y: jnp.where(upwind, x, y)
    r, p, w2 = pick(r_l, r_r), pick(p_l, p_r), pick(w2_l, w2_r)
    inv_r = rcp(r)
    internal = jnp.maximum(2.5 * p * inv_r - 0.25 * r, 0.05)
    drop = (guess - p) * rcp(w2)
    inner = jnp.maximum(internal + 0.5 * (guess + p) * drop, 0.1 * internal)
    mass = u * rcp(inv_r - drop)
    kinetic = u * u
    momenta = []
    for component in (1, 2, 3):
        if component == axis:
            momenta.append(mass * u + guess)
        else:
            carried = pick(left[component], right[component])
            kinetic = kinetic + carried * carried
            momenta.append(mass * carried)
    return [mass] + momenta + [mass * (inner + 0.5 * kinetic) + u * guess]


def z_shift(x, n):
    z = lax.broadcasted_iota(jnp.int32, x.shape, x.ndim - 1) % BZC
    inside = pltpu.roll(x, (-n) % 128, x.ndim - 1)
    around = pltpu.roll(x, ((BZC if n > 0 else -BZC) - n) % 128, x.ndim - 1)
    keep = z < BZC - n if n > 0 else z >= -n
    return jnp.where(keep, inside, around)


def y_shift(x, n):
    lane = lax.broadcasted_iota(jnp.int32, x.shape, 2)
    row = lax.broadcasted_iota(jnp.int32, x.shape, 1)
    turned = pltpu.roll(x, (-n * BZC) % 128, 2)
    moved = pltpu.roll(turned, 7 if n > 0 else 1, 1)
    other = jnp.concatenate([moved[i ^ 1][None] for i in range(x.shape[0])], axis=0)
    carry = jnp.where(row == (7 if n > 0 else 0), other, moved)
    keep = lane < 128 - n * BZC if n > 0 else lane >= -n * BZC
    return jnp.where(keep, turned, carry)


def plane_sweep(q, shift, axis):
    d = [shift(x, 1) - x for x in q]
    d_low = [shift(x, -1) for x in d]
    d_high = [shift(x, 1) for x in d]
    b = [face_offset(l, m, h) for l, m, h in zip(d_low, d, d_high)]
    a = [shift(m - x, -1) for m, x in zip(d, b)]
    p_high = q[4] + (d[4] + d_high[4])
    p_low = shift(q[4], -2)
    chi = shock(d[4] + d_low[4], p_high - p_low, p_high + p_low, -(d[axis] + d_low[axis]))
    flat = 1.0 - jnp.maximum(jnp.maximum(shift(chi, -1), chi), shift(chi, 1))
    pairs = [edges(*x, flat) for x in zip(q, a, b)]
    flux = riemann([shift(x[1], -1) for x in pairs], [x[0] for x in pairs], axis)
    return [shift(x, 1) - x for x in flux]


def step_kernel(
    n, swap_ref, next_ref, cell_ref, out_ref,
    u_ref, first_ref, q_ref, t_ref, a_ref, chi_ref, up_ref, flux_ref, ratio_ref,
    sent_ref, came_ref, fast_ref, fast_in_ref, edge_ref, ghost_ref,
    swap_send, swap_recv, fast_send, fast_recv, edge_send, edge_recv,
):
    depth = out_ref.shape[2]
    chunks = depth // GHOST
    rounds = n.bit_length() - 1
    me = lax.axis_index("box")
    right, left = lax.rem(me + 1, n), lax.rem(me + n - 1, n)
    peers = [me + 2**k * (1 - 2 * lax.rem(lax.div(me, 2**k), 2)) for k in range(rounds)]
    sent_slot = swap_ref[0]
    kept_slot = 1 - sent_slot

    barrier = pltpu.get_barrier_semaphore()
    for peer in peers + [left, right]:
        pl.semaphore_signal(barrier, inc=1, device_id=(peer,), device_id_type=pl.DeviceIdType.MESH)
    pl.semaphore_wait(barrier, rounds + 2)

    def remote(src, dst, send, recv, peer):
        return pltpu.make_async_remote_copy(
            src_ref=src, dst_ref=dst, send_sem=send, recv_sem=recv,
            device_id=(peer,), device_id_type=pl.DeviceIdType.MESH,
        )

    def swap_copy(c):
        part = pl.ds(c * GHOST, GHOST)
        return remote(sent_ref.at[part], came_ref.at[part], swap_send.at[c], swap_recv.at[c], peers[-1])

    def fast_copy(k):
        return remote(fast_ref.at[k], fast_in_ref.at[k], fast_send.at[k], fast_recv.at[k], peers[k])

    def edge_copy(stage, side):
        i = 2 * stage + side
        return remote(edge_ref.at[i], ghost_ref.at[i], edge_send.at[i], edge_recv.at[i], (left, right)[side])

    def chunk(j):
        return lax.rem(j + chunks - 1, chunks)

    def launch(j):
        c = chunk(j)
        for k in range(GHOST):
            x = c * GHOST + k
            for f in range(5):
                sent_ref[x, f] = cell_ref[sent_slot, f, x]
        swap_copy(c).start()

    def arrive(j):
        swap_copy(chunk(j)).wait()

        @pl.when(j + IN_FLIGHT < chunks)
        def _():
            launch(j + IN_FLIGHT)

    pl.loop(0, IN_FLIGHT)(launch)
    fast_ref[0] = jnp.zeros_like(fast_ref[0])

    @pl.loop(0, chunks)
    def _(c):
        speed = signal_speed(primitives([cell_ref[:, f, pl.ds(c * GHOST, GHOST)] for f in range(5)]))
        fast_ref[0] = jnp.maximum(fast_ref[0], jnp.max(speed, axis=(0, 1)))

    def kept(c):
        x = c * GHOST
        u = [cell_ref[kept_slot, f, pl.ds(x, GHOST)] for f in range(5)]
        q = primitives(u)
        dz = plane_sweep(q, z_shift, 3)
        for f in range(5):
            for k in range(GHOST):
                u_ref[f, x + k, 0] = u[f][k]
                q_ref[f, x + GHOST + k, 0] = q[f][k]
                t_ref[f, x + k, 0] = dz[f][k]

    for k in range(rounds):
        fast_copy(k).start()
        pl.loop(chunks * k // rounds, chunks * (k + 1) // rounds)(kept)
        fast_copy(k).wait()
        fast_ref[k + 1] = jnp.maximum(fast_ref[k], fast_in_ref[k])
    ratio_ref[...] = jnp.zeros_like(ratio_ref) + COURANT / jnp.max(fast_ref[rounds], keepdims=True)

    def planes(ref, f, x, m):
        return ref[f, pl.ds(x, m)].reshape(2 * m, 8, 128)

    def put(ref, f, x, m, value):
        ref[f, pl.ds(x, m)] = value.reshape(m, 2, 8, 128)

    def incoming(x):
        u = [came_ref[pl.ds(x, 2), f] for f in range(5)]
        q = primitives(u)
        for f in range(5):
            for k in range(2):
                u_ref[f, x + k, 1] = u[f][k]
                q_ref[f, x + GHOST + k, 1] = q[f][k]
        dz = plane_sweep(q, z_shift, 3)
        dy = plane_sweep([planes(q_ref, f, x + GHOST, 2) for f in range(5)], y_shift, 2)
        for f in range(5):
            along_z = [part[None] for k in range(2) for part in (t_ref[f, x + k, 0], dz[f][k])]
            put(t_ref, f, x, 2, dy[f] + jnp.concatenate(along_z, axis=0))

    def prims(c):
        x = c * GHOST
        q = primitives([planes(first_ref, f, x, GHOST) for f in range(5)])
        for f in range(5):
            put(q_ref, f, x + GHOST, GHOST, q[f])

    def both(x):
        q = [planes(q_ref, f, x + GHOST, 2) for f in range(5)]
        dz = plane_sweep(q, z_shift, 3)
        dy = plane_sweep(q, y_shift, 2)
        for f in range(5):
            put(t_ref, f, x, 2, dz[f] + dy[f])

    def by_slot(pair):
        return jnp.where(sent_slot == 0, pair[1], pair[0]), jnp.where(sent_slot == 0, pair[0], pair[1])

    def send_edge(stage, side, source_ref):
        @pl.loop(0, GHOST)
        def _(k):
            for f in range(5):
                zero, one = by_slot(source_ref[f, k + side * (depth - GHOST)])
                edge_ref[2 * stage + side, 0, k, f] = zero
                edge_ref[2 * stage + side, 1, k, f] = one

        edge_copy(stage, side).start()

    def take_ghosts(stage, side, source_ref):
        edge_copy(stage, 1 - side).wait()
        beside = [next_ref[slot, side] for slot in (kept_slot, sent_slot)]
        base = (left, right)[side] * 2
        own = side * (depth - 1)

        @pl.loop(0, GHOST)
        def _(k):
            u = []
            for f in range(5):
                mine = source_ref[f, own]
                parts = []
                for role in range(2):
                    zero, one = (ghost_ref[2 * stage + 1 - side, slot, k, f] for slot in range(2))
                    theirs = jnp.where(beside[role] == base, zero, one)
                    parts.append(jnp.where(beside[role] < 0, mine[role], theirs)[None])
                u.append(jnp.concatenate(parts, axis=0))
            q = primitives(u)
            for f in range(5):
                q_ref[f, k + side * (depth + GHOST)] = q[f]

    def chi_at(e, m):
        p = [planes(q_ref, 4, e + k, m) for k in (-2, -1, 1, 2)]
        v = [planes(q_ref, 1, e + k, m) for k in (-1, 1)]
        return shock(p[2] - p[1], p[3] - p[0], p[3] + p[0], v[0] - v[1])

    def shifted(first, rest):
        return first if rest.shape[0] == 2 else jnp.concatenate([first, rest[:-2]], axis=0)

    def cell(e, m):
        chi = jnp.concatenate([chi_ref[0], chi_ref[1], chi_at(e + 1, m)], axis=0)
        flat = 1.0 - jnp.maximum(jnp.maximum(chi[:-4], chi[2:-2]), chi[4:])
        chi_ref[0] = chi[-4:-2]
        chi_ref[1] = chi[-2:]
        lower, upper = [], []
        for f in range(5):
            q = [planes(q_ref, f, e + k, m) for k in (-1, 0, 1, 2)]
            d = q[2] - q[1]
            b = face_offset(q[1] - q[0], d, q[3] - q[2])
            a = d - b
            low, high = edges(q[1], shifted(a_ref[f], a), b, flat)
            a_ref[f] = a[-2:]
            lower.append(low)
            upper.append(high)
        return lower, upper

    def face(e, m):
        lower, upper = cell(e, m)
        flux = riemann([shifted(up_ref[f], upper[f]) for f in range(5)], lower, 1)
        for f in range(5):
            up_ref[f] = upper[f][-2:]
        return flux

    def begin_x():
        for f in range(5):
            q = [q_ref[f, k] for k in (1, 2, 3, 4)]
            d = q[2] - q[1]
            a_ref[f] = d - face_offset(q[1] - q[0], d, q[3] - q[2])
        chi_ref[0] = chi_at(2, 1)
        chi_ref[1] = chi_at(3, 1)
        _, upper = cell(3, 1)
        for f in range(5):
            up_ref[f] = upper[f]
        flux = face(GHOST, 1)
        for f in range(5):
            flux_ref[f] = flux[f]

    def rate_x(x):
        flux = face(x + GHOST + 1, XSTEP)
        rate = []
        for f in range(5):
            change = flux[f] - shifted(flux_ref[f], flux[f]) + planes(t_ref, f, x, XSTEP)
            rate.append(ratio_ref[...] * change)
            flux_ref[f] = flux[f][-2:]
        return rate

    def first_x(x):
        rate = rate_x(x)
        for f in range(5):
            put(first_ref, f, x, XSTEP, planes(u_ref, f, x, XSTEP) - rate[f])

    def last_x(x):
        rate = rate_x(x)
        for f in range(5):
            new = 0.5 * (planes(u_ref, f, x, XSTEP) + (planes(first_ref, f, x, XSTEP) - rate[f]))
            for k in range(XSTEP):
                zero, one = by_slot(new[2 * k : 2 * k + 2])
                out_ref[0, f, x + k] = zero
                out_ref[1, f, x + k] = one

    arrive(0)
    arrive(1)
    pl.loop(0, GHOST)(lambda j: incoming(lax.rem(2 * j + depth - GHOST, depth)))
    send_edge(0, 1, u_ref)
    send_edge(0, 0, u_ref)

    def middle(c):
        arrive(c + 1)
        pl.loop(0, GHOST // 2)(lambda k: incoming(c * GHOST + 2 * k))

    middle(1)
    take_ghosts(0, 0, u_ref)
    begin_x()
    pl.loop(0, GHOST, step=XSTEP)(first_x)

    @pl.loop(2, chunks - 1)
    def _(c):
        middle(c)
        pl.loop(0, GHOST, step=XSTEP)(lambda k: first_x(c * GHOST - GHOST + k))

    take_ghosts(0, 1, u_ref)
    pl.loop(depth - 2 * GHOST, depth, step=XSTEP)(first_x)
    send_edge(1, 0, first_ref)
    send_edge(1, 1, first_ref)
    pl.loop(0, chunks)(prims)
    pl.loop(0, LEAD, step=2)(both)
    take_ghosts(1, 0, first_ref)
    take_ghosts(1, 1, first_ref)
    begin_x()

    @pl.loop(0, depth - LEAD, step=2)
    def _(x):
        last_x(x)
        both(x + LEAD)

    pl.loop(depth - LEAD, depth, step=XSTEP)(last_x)


def body(cell_state, swap_slots, neighbours):
    slots, fields, depth, _ = cell_state.shape
    n = lax.axis_size("box")
    rounds = n.bit_length() - 1
    cells = cell_state.reshape(slots, fields, depth, 8, 128)
    vmem, smem = (pl.BlockSpec(memory_space=space) for space in (pltpu.VMEM, pltpu.SMEM))
    pair = (slots, 8, 128)
    tile = (8, 128)
    scratch = [
        (fields, depth) + pair,
        (fields, depth) + pair,
        (fields, depth + 2 * GHOST) + pair,
        (fields, depth) + pair,
        (fields,) + pair,
        (2,) + pair,
        (fields,) + pair,
        (fields,) + pair,
        tile,
        (depth, fields) + tile,
        (depth, fields) + tile,
        (rounds + 1,) + tile,
        (rounds,) + tile,
        (4, slots, GHOST, fields) + tile,
        (4, slots, GHOST, fields) + tile,
    ]
    counts = [depth // GHOST] * 2 + [rounds] * 2 + [4] * 2
    new = pl.pallas_call(
        functools.partial(step_kernel, n),
        out_shape=jax.ShapeDtypeStruct(cells.shape, jnp.float32),
        in_specs=[smem, smem, vmem],
        out_specs=vmem,
        scratch_shapes=[pltpu.VMEM(s, jnp.float32) for s in scratch]
        + [pltpu.SemaphoreType.DMA((k,)) for k in counts],
        compiler_params=pltpu.CompilerParams(
            vmem_limit_bytes=40 * 2**20, collective_id=0, has_side_effects=True
        ),
    )(swap_slots, neighbours, cells)
    return new.reshape(cell_state.shape)


def solution(mesh):
    in_specs = (P("box", None, None, None), P("box"), P("box", None))
    out_specs = P("box", None, None, None)
    return jax.shard_map(body, mesh=mesh, in_specs=in_specs, out_specs=out_specs, check_vma=False)
```

```python
import functools

import jax
import jax.numpy as jnp
from jax import lax
from jax.experimental import pallas as pl
from jax.experimental.pallas import tpu as pltpu
from jax.sharding import PartitionSpec as P

BZC = 32
GHOST = 4
RIEMANN_ITERS = 3
COURANT = 0.4
XSTEP = 2
IN_FLIGHT = 3
LAST_XSTEP = 4


def rcp(x):
    return pl.reciprocal(x, approx=True)


def primitives(u):
    density = jnp.maximum(u[0], 0.05)
    inv = 1.0 / density
    v1, v2, v3 = u[1] * inv, u[2] * inv, u[3] * inv
    internal = jnp.maximum(u[4] * inv - 0.5 * (v1 * v1 + v2 * v2 + v3 * v3), 0.05)
    pressure = density * (0.4 * internal + 0.1 * density)
    return density, v1, v2, v3, pressure


def signal_speed(q):
    sound = jnp.sqrt(0.1 * q[0] + 1.4 * q[4] / q[0])
    return jnp.abs(q[1]) + jnp.abs(q[2]) + jnp.abs(q[3]) + 3.0 * sound


def clip_to(x, span):
    return jnp.minimum(jnp.maximum(x, jnp.minimum(span, 0.0)), jnp.maximum(span, 0.0))


def face_offset(d_low, d, d_high):
    return clip_to(0.5 * d + (d_low - d_high) * (1.0 / 12.0), d)


def shock(near, far, far_sum, squeeze):
    steep = jnp.abs(near) * rcp(jnp.abs(far) + 0.1 * far_sum)
    squeeze = jnp.maximum(squeeze, 0.0)
    return jnp.clip(4.0 * steep - 3.0, 0.0, 1.0) * squeeze * rcp(squeeze + 0.2)


def edges(q, a, b, flat):
    lower = q - flat * clip_to(b + b, a)
    upper = q + flat * clip_to(a + a, b)
    return lower, upper


def wave_side(r, p):
    t = 0.1 * r * r
    c2 = r * (t + 1.4 * p)
    slope = 0.5 * r * (2.4 + t * rcp(p))
    return c2, slope, c2 - slope * p


def riemann(left, right, axis):
    r_l, u_l, p_l = left[0], left[axis], left[4]
    r_r, u_r, p_r = right[0], right[axis], right[4]
    c2_l, b_l, a_l = wave_side(r_l, p_l)
    c2_r, b_r, a_r = wave_side(r_r, p_r)
    c_l = c2_l * lax.rsqrt(c2_l)
    c_r = c2_r * lax.rsqrt(c2_r)
    floor_p = 0.1 * jnp.minimum(p_l, p_r)
    guess = (c_r * p_l + c_l * p_r + c_l * c_r * (u_l - u_r)) * rcp(c_l + c_r)
    guess = jnp.maximum(guess, floor_p)
    for _ in range(RIEMANN_ITERS):
        i_l = lax.rsqrt(a_l + b_l * guess)
        i_r = lax.rsqrt(a_r + b_r * guess)
        star_l = u_l - (guess - p_l) * i_l
        star_r = u_r + (guess - p_r) * i_r
        y_l = i_l + i_l * (c2_l * (i_l * i_l))
        y_r = i_r + i_r * (c2_r * (i_r * i_r))
        guess = jnp.maximum(guess - 2.0 * (star_r - star_l) * rcp(y_l + y_r), floor_p)
    w2_l = a_l + b_l * guess
    w2_r = a_r + b_r * guess
    w_l = w2_l * lax.rsqrt(w2_l)
    w_r = w2_r * lax.rsqrt(w2_r)
    u = (w_l * u_l + w_r * u_r + (p_l - p_r)) * rcp(w_l + w_r)
    upwind = u >= 0.0
    pick = lambda x, y: jnp.where(upwind, x, y)
    r, p, w2 = pick(r_l, r_r), pick(p_l, p_r), pick(w2_l, w2_r)
    inv_r = rcp(r)
    internal = jnp.maximum(2.5 * p * inv_r - 0.25 * r, 0.05)
    drop = (guess - p) * rcp(w2)
    inner = jnp.maximum(internal + 0.5 * (guess + p) * drop, 0.1 * internal)
    mass = u * rcp(inv_r - drop)
    kinetic = u * u
    momenta = []
    for component in (1, 2, 3):
        if component == axis:
            momenta.append(mass * u + guess)
        else:
            carried = pick(left[component], right[component])
            kinetic = kinetic + carried * carried
            momenta.append(mass * carried)
    return [mass] + momenta + [mass * (inner + 0.5 * kinetic) + u * guess]


def z_shift(x, n):
    z = lax.broadcasted_iota(jnp.int32, x.shape, x.ndim - 1) % BZC
    inside = pltpu.roll(x, (-n) % 128, x.ndim - 1)
    around = pltpu.roll(x, ((BZC if n > 0 else -BZC) - n) % 128, x.ndim - 1)
    keep = z < BZC - n if n > 0 else z >= -n
    return jnp.where(keep, inside, around)


def y_shift(x, n):
    lane = lax.broadcasted_iota(jnp.int32, x.shape, 2)
    row = lax.broadcasted_iota(jnp.int32, x.shape, 1)
    turned = pltpu.roll(x, (-n * BZC) % 128, 2)
    moved = pltpu.roll(turned, 7 if n > 0 else 1, 1)
    other = jnp.concatenate([moved[i ^ 1][None] for i in range(x.shape[0])], axis=0)
    carry = jnp.where(row == (7 if n > 0 else 0), other, moved)
    keep = lane < 128 - n * BZC if n > 0 else lane >= -n * BZC
    return jnp.where(keep, turned, carry)


def plane_sweep(q, shift, axis):
    d = [shift(x, 1) - x for x in q]
    d_low = [shift(x, -1) for x in d]
    d_high = [shift(x, 1) for x in d]
    b = [face_offset(l, m, h) for l, m, h in zip(d_low, d, d_high)]
    a = [shift(m - x, -1) for m, x in zip(d, b)]
    p_high = q[4] + (d[4] + d_high[4])
    p_low = shift(q[4], -2)
    chi = shock(d[4] + d_low[4], p_high - p_low, p_high + p_low, -(d[axis] + d_low[axis]))
    flat = 1.0 - jnp.maximum(jnp.maximum(shift(chi, -1), chi), shift(chi, 1))
    pairs = [edges(*x, flat) for x in zip(q, a, b)]
    flux = riemann([shift(x[1], -1) for x in pairs], [x[0] for x in pairs], axis)
    return [shift(x, 1) - x for x in flux]


def step_kernel(
    n, swap_ref, next_ref, cell_ref, out_ref,
    u_ref, first_ref, q_ref, t_ref, q_two_ref, t_two_ref, a_ref, chi_ref, up_ref, flux_ref, ratio_ref,
    sent_ref, came_ref, fast_ref, fast_in_ref, edge_ref, ghost_ref,
    swap_send, swap_recv, fast_send, fast_recv, edge_send, edge_recv,
):
    depth = out_ref.shape[2]
    chunks = depth // GHOST
    rounds = n.bit_length() - 1
    me = lax.axis_index("box")
    right, left = lax.rem(me + 1, n), lax.rem(me + n - 1, n)
    peers = [me + 2**k * (1 - 2 * lax.rem(lax.div(me, 2**k), 2)) for k in range(rounds)]
    sent_slot = swap_ref[0]
    kept_slot = 1 - sent_slot

    barrier = pltpu.get_barrier_semaphore()
    for peer in peers + [left, right]:
        pl.semaphore_signal(barrier, inc=1, device_id=(peer,), device_id_type=pl.DeviceIdType.MESH)
    pl.semaphore_wait(barrier, rounds + 2)

    def remote(src, dst, send, recv, peer):
        return pltpu.make_async_remote_copy(
            src_ref=src, dst_ref=dst, send_sem=send, recv_sem=recv,
            device_id=(peer,), device_id_type=pl.DeviceIdType.MESH,
        )

    def swap_copy(c):
        part = pl.ds(c * GHOST, GHOST)
        return remote(sent_ref.at[part], came_ref.at[part], swap_send.at[c], swap_recv.at[c], peers[-1])

    def fast_copy(k):
        return remote(fast_ref.at[k], fast_in_ref.at[k], fast_send.at[k], fast_recv.at[k], peers[k])

    def edge_copy(stage, side):
        i = 2 * stage + side
        return remote(edge_ref.at[i], ghost_ref.at[i], edge_send.at[i], edge_recv.at[i], (left, right)[side])

    def chunk(j):
        return lax.rem(j + chunks - 1, chunks)

    def launch(j):
        c = chunk(j)
        for k in range(GHOST):
            x = c * GHOST + k
            for f in range(5):
                sent_ref[x, f] = cell_ref[sent_slot, f, x]
        swap_copy(c).start()

    def arrive(j):
        swap_copy(chunk(j)).wait()

        @pl.when(j + IN_FLIGHT < chunks)
        def _():
            launch(j + IN_FLIGHT)

    pl.loop(0, IN_FLIGHT)(launch)
    fast_ref[0] = jnp.zeros_like(fast_ref[0])

    @pl.loop(0, chunks)
    def _(c):
        speed = signal_speed(primitives([cell_ref[:, f, pl.ds(c * GHOST, GHOST)] for f in range(5)]))
        fast_ref[0] = jnp.maximum(fast_ref[0], jnp.max(speed, axis=(0, 1)))

    def kept(c):
        x = c * GHOST
        u = [cell_ref[kept_slot, f, pl.ds(x, GHOST)] for f in range(5)]
        q = primitives(u)
        dz = plane_sweep(q, z_shift, 3)
        for f in range(5):
            for k in range(GHOST):
                u_ref[f, x + k, 0] = u[f][k]
                q_ref[f, x + GHOST + k, 0] = q[f][k]
                t_ref[f, x + k, 0] = dz[f][k]

    for k in range(rounds):
        fast_copy(k).start()
        pl.loop(chunks * k // rounds, chunks * (k + 1) // rounds)(kept)
        fast_copy(k).wait()
        fast_ref[k + 1] = jnp.maximum(fast_ref[k], fast_in_ref[k])
    ratio_ref[...] = jnp.zeros_like(ratio_ref) + COURANT / jnp.max(fast_ref[rounds], keepdims=True)

    def planes(ref, f, x, m):
        return ref[f, pl.ds(x, m)].reshape(2 * m, 8, 128)

    def put(ref, f, x, m, value):
        ref[f, pl.ds(x, m)] = value.reshape(m, 2, 8, 128)

    def incoming(x):
        u = [came_ref[pl.ds(x, 2), f] for f in range(5)]
        q = primitives(u)
        for f in range(5):
            for k in range(2):
                u_ref[f, x + k, 1] = u[f][k]
                q_ref[f, x + GHOST + k, 1] = q[f][k]
        dz = plane_sweep(q, z_shift, 3)
        dy = plane_sweep([planes(q_ref, f, x + GHOST, 2) for f in range(5)], y_shift, 2)
        for f in range(5):
            along_z = [part[None] for k in range(2) for part in (t_ref[f, x + k, 0], dz[f][k])]
            put(t_ref, f, x, 2, dy[f] + jnp.concatenate(along_z, axis=0))

    def second(x):
        q = primitives([planes(first_ref, f, x, 2) for f in range(5)])
        for f in range(5):
            put(q_two_ref, f, x + GHOST, 2, q[f])
        dz = plane_sweep(q, z_shift, 3)
        dy = plane_sweep(q, y_shift, 2)
        for f in range(5):
            put(t_two_ref, f, x, 2, dz[f] + dy[f])

    def by_slot(pair):
        return jnp.where(sent_slot == 0, pair[1], pair[0]), jnp.where(sent_slot == 0, pair[0], pair[1])

    def send_edge(stage, side, source_ref):
        @pl.loop(0, GHOST)
        def _(k):
            for f in range(5):
                zero, one = by_slot(source_ref[f, k + side * (depth - GHOST)])
                edge_ref[2 * stage + side, 0, k, f] = zero
                edge_ref[2 * stage + side, 1, k, f] = one

        edge_copy(stage, side).start()

    prim_refs = (q_ref, q_two_ref)

    def take_ghosts(stage, side, source_ref):
        edge_copy(stage, 1 - side).wait()
        beside = [next_ref[slot, side] for slot in (kept_slot, sent_slot)]
        base = (left, right)[side] * 2
        own = side * (depth - 1)

        @pl.loop(0, GHOST)
        def _(k):
            u = []
            for f in range(5):
                mine = source_ref[f, own]
                parts = []
                for role in range(2):
                    zero, one = (ghost_ref[2 * stage + 1 - side, slot, k, f] for slot in range(2))
                    theirs = jnp.where(beside[role] == base, zero, one)
                    parts.append(jnp.where(beside[role] < 0, mine[role], theirs)[None])
                u.append(jnp.concatenate(parts, axis=0))
            q = primitives(u)
            for f in range(5):
                prim_refs[stage][f, k + side * (depth + GHOST)] = q[f]

    def chi_at(prim_ref, e, m):
        p = [planes(prim_ref, 4, e + k, m) for k in (-2, -1, 1, 2)]
        v = [planes(prim_ref, 1, e + k, m) for k in (-1, 1)]
        return shock(p[2] - p[1], p[3] - p[0], p[3] + p[0], v[0] - v[1])

    def shifted(first, rest):
        return first if rest.shape[0] == 2 else jnp.concatenate([first, rest[:-2]], axis=0)

    def cell(prim_ref, e, m):
        chi = jnp.concatenate([chi_ref[0], chi_ref[1], chi_at(prim_ref, e + 1, m)], axis=0)
        flat = 1.0 - jnp.maximum(jnp.maximum(chi[:-4], chi[2:-2]), chi[4:])
        chi_ref[0] = chi[-4:-2]
        chi_ref[1] = chi[-2:]
        lower, upper = [], []
        for f in range(5):
            q = [planes(prim_ref, f, e + k, m) for k in (-1, 0, 1, 2)]
            d = q[2] - q[1]
            b = face_offset(q[1] - q[0], d, q[3] - q[2])
            a = d - b
            low, high = edges(q[1], shifted(a_ref[f], a), b, flat)
            a_ref[f] = a[-2:]
            lower.append(low)
            upper.append(high)
        return lower, upper

    def face(prim_ref, e, m):
        lower, upper = cell(prim_ref, e, m)
        flux = riemann([shifted(up_ref[f], upper[f]) for f in range(5)], lower, 1)
        for f in range(5):
            up_ref[f] = upper[f][-2:]
        return flux

    def begin_x(prim_ref):
        for f in range(5):
            q = [prim_ref[f, k] for k in (1, 2, 3, 4)]
            d = q[2] - q[1]
            a_ref[f] = d - face_offset(q[1] - q[0], d, q[3] - q[2])
        chi_ref[0] = chi_at(prim_ref, 2, 1)
        chi_ref[1] = chi_at(prim_ref, 3, 1)
        _, upper = cell(prim_ref, 3, 1)
        for f in range(5):
            up_ref[f] = upper[f]
        flux = face(prim_ref, GHOST, 1)
        for f in range(5):
            flux_ref[f] = flux[f]

    def rate_x(prim_ref, rest_ref, x, m):
        flux = face(prim_ref, x + GHOST + 1, m)
        rate = []
        for f in range(5):
            change = flux[f] - shifted(flux_ref[f], flux[f]) + planes(rest_ref, f, x, m)
            rate.append(ratio_ref[...] * change)
            flux_ref[f] = flux[f][-2:]
        return rate

    def first_x(x):
        rate = rate_x(q_ref, t_ref, x, XSTEP)
        for f in range(5):
            put(first_ref, f, x, XSTEP, planes(u_ref, f, x, XSTEP) - rate[f])

    def last_x(x):
        rate = rate_x(q_two_ref, t_two_ref, x, LAST_XSTEP)
        for f in range(5):
            new = 0.5 * (planes(u_ref, f, x, LAST_XSTEP) + (planes(first_ref, f, x, LAST_XSTEP) - rate[f]))
            for k in range(LAST_XSTEP):
                zero, one = by_slot(new[2 * k : 2 * k + 2])
                out_ref[0, f, x + k] = zero
                out_ref[1, f, x + k] = one

    arrive(0)
    arrive(1)
    pl.loop(0, GHOST)(lambda j: incoming(lax.rem(2 * j + depth - GHOST, depth)))
    send_edge(0, 1, u_ref)
    send_edge(0, 0, u_ref)

    def middle(c):
        arrive(c + 1)
        pl.loop(0, GHOST // 2)(lambda k: incoming(c * GHOST + 2 * k))

    middle(1)
    take_ghosts(0, 0, u_ref)
    begin_x(q_ref)
    pl.loop(0, GHOST, step=XSTEP)(first_x)

    @pl.loop(2, chunks - 1)
    def _(c):
        middle(c)

        @pl.loop(c * GHOST - GHOST, c * GHOST, step=XSTEP)
        def _(x):
            first_x(x)
            second(x - GHOST)

    send_edge(1, 0, first_ref)
    take_ghosts(0, 1, u_ref)
    pl.loop(depth - 2 * GHOST, depth, step=XSTEP)(first_x)
    send_edge(1, 1, first_ref)
    pl.loop(depth - 3 * GHOST, depth, step=2)(second)
    take_ghosts(1, 0, first_ref)
    take_ghosts(1, 1, first_ref)
    begin_x(q_two_ref)
    pl.loop(0, depth, step=LAST_XSTEP)(last_x)


def body(cell_state, swap_slots, neighbours):
    slots, fields, depth, _ = cell_state.shape
    n = lax.axis_size("box")
    rounds = n.bit_length() - 1
    cells = cell_state.reshape(slots, fields, depth, 8, 128)
    vmem, smem = (pl.BlockSpec(memory_space=space) for space in (pltpu.VMEM, pltpu.SMEM))
    pair = (slots, 8, 128)
    tile = (8, 128)
    scratch = [
        (fields, depth) + pair,
        (fields, depth) + pair,
        (fields, depth + 2 * GHOST) + pair,
        (fields, depth) + pair,
        (fields, depth + 2 * GHOST) + pair,
        (fields, depth) + pair,
        (fields,) + pair,
        (2,) + pair,
        (fields,) + pair,
        (fields,) + pair,
        tile,
        (depth, fields) + tile,
        (depth, fields) + tile,
        (rounds + 1,) + tile,
        (rounds,) + tile,
        (4, slots, GHOST, fields) + tile,
        (4, slots, GHOST, fields) + tile,
    ]
    counts = [depth // GHOST] * 2 + [rounds] * 2 + [4] * 2
    new = pl.pallas_call(
        functools.partial(step_kernel, n),
        out_shape=jax.ShapeDtypeStruct(cells.shape, jnp.float32),
        in_specs=[smem, smem, vmem],
        out_specs=vmem,
        scratch_shapes=[pltpu.VMEM(s, jnp.float32) for s in scratch]
        + [pltpu.SemaphoreType.DMA((k,)) for k in counts],
        compiler_params=pltpu.CompilerParams(
            vmem_limit_bytes=40 * 2**20, collective_id=0, has_side_effects=True
        ),
    )(swap_slots, neighbours, cells)
    return new.reshape(cell_state.shape)


def solution(mesh):
    in_specs = (P("box", None, None, None), P("box"), P("box", None))
    out_specs = P("box", None, None, None)
    return jax.shard_map(body, mesh=mesh, in_specs=in_specs, out_specs=out_specs, check_vma=False)
```

```python
import functools

import jax
import jax.numpy as jnp
from jax import lax
from jax.experimental import pallas as pl
from jax.experimental.pallas import tpu as pltpu
from jax.sharding import PartitionSpec as P

BZC = 32
GHOST = 4
RIEMANN_ITERS = 3
COURANT = 0.4
XSTEP = 2
IN_FLIGHT = 3
LAST_XSTEP = 4


def rcp(x):
    return pl.reciprocal(x, approx=True)


def primitives(u):
    density = jnp.maximum(u[0], 0.05)
    inv = 1.0 / density
    v1, v2, v3 = u[1] * inv, u[2] * inv, u[3] * inv
    internal = jnp.maximum(u[4] * inv - 0.5 * (v1 * v1 + v2 * v2 + v3 * v3), 0.05)
    pressure = density * (0.4 * internal + 0.1 * density)
    return density, v1, v2, v3, pressure


def signal_speed(q):
    sound = jnp.sqrt(0.1 * q[0] + 1.4 * q[4] / q[0])
    return jnp.abs(q[1]) + jnp.abs(q[2]) + jnp.abs(q[3]) + 3.0 * sound


def clip_to(x, span):
    return jnp.minimum(jnp.maximum(x, jnp.minimum(span, 0.0)), jnp.maximum(span, 0.0))


def face_offset(d_low, d, d_high):
    return clip_to(0.5 * d + (d_low - d_high) * (1.0 / 12.0), d)


def shock(near, far, far_sum, squeeze):
    steep = jnp.abs(near) * rcp(jnp.abs(far) + 0.1 * far_sum)
    squeeze = jnp.maximum(squeeze, 0.0)
    return jnp.clip(4.0 * steep - 3.0, 0.0, 1.0) * squeeze * rcp(squeeze + 0.2)


def edges(q, a, b, flat):
    lower = q - flat * clip_to(b + b, a)
    upper = q + flat * clip_to(a + a, b)
    return lower, upper


def wave_side(r, p):
    t = 0.1 * r * r
    c2 = r * (t + 1.4 * p)
    slope = 0.5 * r * (2.4 + t * rcp(p))
    return c2, slope, c2 - slope * p


def riemann(left, right, axis):
    r_l, u_l, p_l = left[0], left[axis], left[4]
    r_r, u_r, p_r = right[0], right[axis], right[4]
    c2_l, b_l, a_l = wave_side(r_l, p_l)
    c2_r, b_r, a_r = wave_side(r_r, p_r)
    c_l = c2_l * lax.rsqrt(c2_l)
    c_r = c2_r * lax.rsqrt(c2_r)
    floor_p = 0.1 * jnp.minimum(p_l, p_r)
    guess = (c_r * p_l + c_l * p_r + c_l * c_r * (u_l - u_r)) * rcp(c_l + c_r)
    guess = jnp.maximum(guess, floor_p)
    apart = u_r - u_l
    half_l, half_r = 0.5 * c2_l, 0.5 * c2_r
    for _ in range(RIEMANN_ITERS):
        i_l = lax.rsqrt(a_l + b_l * guess)
        i_r = lax.rsqrt(a_r + b_r * guess)
        gap = apart + (guess - p_r) * i_r + (guess - p_l) * i_l
        y_l = i_l * (0.5 + half_l * (i_l * i_l))
        y_r = i_r * (0.5 + half_r * (i_r * i_r))
        guess = jnp.maximum(guess - gap * rcp(y_l + y_r), floor_p)
    w2_l = a_l + b_l * guess
    w2_r = a_r + b_r * guess
    w_l = w2_l * lax.rsqrt(w2_l)
    w_r = w2_r * lax.rsqrt(w2_r)
    u = (w_l * u_l + w_r * u_r + (p_l - p_r)) * rcp(w_l + w_r)
    upwind = u >= 0.0
    pick = lambda x, y: jnp.where(upwind, x, y)
    r, p, w2 = pick(r_l, r_r), pick(p_l, p_r), pick(w2_l, w2_r)
    inv_r = rcp(r)
    internal = jnp.maximum(2.5 * p * inv_r - 0.25 * r, 0.05)
    drop = (guess - p) * rcp(w2)
    inner = jnp.maximum(internal + 0.5 * (guess + p) * drop, 0.1 * internal)
    mass = u * rcp(inv_r - drop)
    kinetic = u * u
    momenta = []
    for component in (1, 2, 3):
        if component == axis:
            momenta.append(mass * u + guess)
        else:
            carried = pick(left[component], right[component])
            kinetic = kinetic + carried * carried
            momenta.append(mass * carried)
    return [mass] + momenta + [mass * (inner + 0.5 * kinetic) + u * guess]


def z_shift(shape):
    z = lax.broadcasted_iota(jnp.int32, shape, 2) & (BZC - 1)
    keep = {1: z < BZC - 1, -1: z >= 1, -2: z >= 2}

    def shift(x, n):
        inside = pltpu.roll(x, (-n) % 128, 2)
        around = pltpu.roll(x, ((BZC if n > 0 else -BZC) - n) % 128, 2)
        return jnp.where(keep[n], inside, around)

    return shift


def y_shift(shape):
    lane = lax.broadcasted_iota(jnp.int32, shape, 2)
    row = lax.broadcasted_iota(jnp.int32, shape, 1)
    keep = {1: lane < 128 - BZC, -1: lane >= BZC, -2: lane >= 2 * BZC}
    first, last = row == 0, row == 7

    def shift(x, n):
        turned = pltpu.roll(x, (-n * BZC) % 128, 2)
        moved = pltpu.roll(turned, 7 if n > 0 else 1, 1)
        other = jnp.concatenate([moved[i ^ 1][None] for i in range(shape[0])], axis=0)
        carry = jnp.where(last if n > 0 else first, other, moved)
        return jnp.where(keep[n], turned, carry)

    return shift


def plane_sweep(q, shift_of, axis):
    shift = shift_of(q[0].shape)
    d = [shift(x, 1) - x for x in q]
    d_low = [shift(x, -1) for x in d]
    d_high = [shift(x, 1) for x in d]
    b = [face_offset(l, m, h) for l, m, h in zip(d_low, d, d_high)]
    a = [shift(m - x, -1) for m, x in zip(d, b)]
    p_high = q[4] + (d[4] + d_high[4])
    p_low = shift(q[4], -2)
    chi = shock(d[4] + d_low[4], p_high - p_low, p_high + p_low, -(d[axis] + d_low[axis]))
    flat = 1.0 - jnp.maximum(jnp.maximum(shift(chi, -1), chi), shift(chi, 1))
    pairs = [edges(*x, flat) for x in zip(q, a, b)]
    flux = riemann([shift(x[1], -1) for x in pairs], [x[0] for x in pairs], axis)
    return [shift(x, 1) - x for x in flux]


def step_kernel(
    n, swap_ref, next_ref, cell_ref, out_ref,
    u_ref, first_ref, q_ref, t_ref, q_two_ref, t_two_ref, a_ref, chi_ref, up_ref, flux_ref, ratio_ref,
    sent_ref, came_ref, fast_ref, fast_in_ref, edge_ref, ghost_ref,
    swap_send, swap_recv, fast_send, fast_recv, edge_send, edge_recv,
):
    depth = out_ref.shape[2]
    chunks = depth // GHOST
    rounds = n.bit_length() - 1
    me = lax.axis_index("box")
    right, left = lax.rem(me + 1, n), lax.rem(me + n - 1, n)
    peers = [me + 2**k * (1 - 2 * lax.rem(lax.div(me, 2**k), 2)) for k in range(rounds)]
    sent_slot = swap_ref[0]
    kept_slot = 1 - sent_slot

    barrier = pltpu.get_barrier_semaphore()
    for peer in peers + [left, right]:
        pl.semaphore_signal(barrier, inc=1, device_id=(peer,), device_id_type=pl.DeviceIdType.MESH)
    pl.semaphore_wait(barrier, rounds + 2)

    def remote(src, dst, send, recv, peer):
        return pltpu.make_async_remote_copy(
            src_ref=src, dst_ref=dst, send_sem=send, recv_sem=recv,
            device_id=(peer,), device_id_type=pl.DeviceIdType.MESH,
        )

    def swap_copy(c):
        part = pl.ds(c * GHOST, GHOST)
        return remote(sent_ref.at[part], came_ref.at[part], swap_send.at[c], swap_recv.at[c], peers[-1])

    def fast_copy(k):
        return remote(fast_ref.at[k], fast_in_ref.at[k], fast_send.at[k], fast_recv.at[k], peers[k])

    def edge_copy(stage, side):
        i = 2 * stage + side
        return remote(edge_ref.at[i], ghost_ref.at[i], edge_send.at[i], edge_recv.at[i], (left, right)[side])

    def chunk(j):
        return lax.rem(j + chunks - 1, chunks)

    def launch(j):
        c = chunk(j)
        for k in range(GHOST):
            x = c * GHOST + k
            for f in range(5):
                sent_ref[x, f] = cell_ref[sent_slot, f, x]
        swap_copy(c).start()

    def arrive(j):
        swap_copy(chunk(j)).wait()

        @pl.when(j + IN_FLIGHT < chunks)
        def _():
            launch(j + IN_FLIGHT)

    pl.loop(0, IN_FLIGHT)(launch)
    fast_ref[0] = jnp.zeros_like(fast_ref[0])

    @pl.loop(0, chunks)
    def _(c):
        speed = signal_speed(primitives([cell_ref[:, f, pl.ds(c * GHOST, GHOST)] for f in range(5)]))
        fast_ref[0] = jnp.maximum(fast_ref[0], jnp.max(speed, axis=(0, 1)))

    def kept(c):
        x = c * GHOST
        u = [cell_ref[kept_slot, f, pl.ds(x, GHOST)] for f in range(5)]
        q = primitives(u)
        dz = plane_sweep(q, z_shift, 3)
        for f in range(5):
            for k in range(GHOST):
                u_ref[f, x + k, 0] = u[f][k]
                q_ref[f, x + GHOST + k, 0] = q[f][k]
                t_ref[f, x + k, 0] = dz[f][k]

    for k in range(rounds):
        fast_copy(k).start()
        pl.loop(chunks * k // rounds, chunks * (k + 1) // rounds)(kept)
        fast_copy(k).wait()
        fast_ref[k + 1] = jnp.maximum(fast_ref[k], fast_in_ref[k])
    ratio_ref[...] = jnp.zeros_like(ratio_ref) + COURANT / jnp.max(fast_ref[rounds], keepdims=True)

    def planes(ref, f, x, m):
        return ref[f, pl.ds(x, m)].reshape(2 * m, 8, 128)

    def put(ref, f, x, m, value):
        ref[f, pl.ds(x, m)] = value.reshape(m, 2, 8, 128)

    def incoming(x):
        u = [came_ref[pl.ds(x, 2), f] for f in range(5)]
        q = primitives(u)
        for f in range(5):
            for k in range(2):
                u_ref[f, x + k, 1] = u[f][k]
                q_ref[f, x + GHOST + k, 1] = q[f][k]
        dz = plane_sweep(q, z_shift, 3)
        dy = plane_sweep([planes(q_ref, f, x + GHOST, 2) for f in range(5)], y_shift, 2)
        for f in range(5):
            along_z = [part[None] for k in range(2) for part in (t_ref[f, x + k, 0], dz[f][k])]
            put(t_ref, f, x, 2, dy[f] + jnp.concatenate(along_z, axis=0))

    def second(x):
        q = primitives([planes(first_ref, f, x, 2) for f in range(5)])
        for f in range(5):
            put(q_two_ref, f, x + GHOST, 2, q[f])
        dz = plane_sweep(q, z_shift, 3)
        dy = plane_sweep(q, y_shift, 2)
        for f in range(5):
            put(t_two_ref, f, x, 2, dz[f] + dy[f])

    def by_slot(pair):
        return jnp.where(sent_slot == 0, pair[1], pair[0]), jnp.where(sent_slot == 0, pair[0], pair[1])

    def send_edge(stage, side, source_ref):
        @pl.loop(0, GHOST)
        def _(k):
            for f in range(5):
                zero, one = by_slot(source_ref[f, k + side * (depth - GHOST)])
                edge_ref[2 * stage + side, 0, k, f] = zero
                edge_ref[2 * stage + side, 1, k, f] = one

        edge_copy(stage, side).start()

    prim_refs = (q_ref, q_two_ref)

    def take_ghosts(stage, side, source_ref):
        edge_copy(stage, 1 - side).wait()
        beside = [next_ref[slot, side] for slot in (kept_slot, sent_slot)]
        base = (left, right)[side] * 2
        own = side * (depth - 1)

        @pl.loop(0, GHOST)
        def _(k):
            u = []
            for f in range(5):
                mine = source_ref[f, own]
                parts = []
                for role in range(2):
                    zero, one = (ghost_ref[2 * stage + 1 - side, slot, k, f] for slot in range(2))
                    theirs = jnp.where(beside[role] == base, zero, one)
                    parts.append(jnp.where(beside[role] < 0, mine[role], theirs)[None])
                u.append(jnp.concatenate(parts, axis=0))
            q = primitives(u)
            for f in range(5):
                prim_refs[stage][f, k + side * (depth + GHOST)] = q[f]

    def chi_at(prim_ref, e, m):
        p = [planes(prim_ref, 4, e + k, m) for k in (-2, -1, 1, 2)]
        v = [planes(prim_ref, 1, e + k, m) for k in (-1, 1)]
        return shock(p[2] - p[1], p[3] - p[0], p[3] + p[0], v[0] - v[1])

    def shifted(first, rest):
        return first if rest.shape[0] == 2 else jnp.concatenate([first, rest[:-2]], axis=0)

    def cell(prim_ref, e, m):
        chi = jnp.concatenate([chi_ref[0], chi_ref[1], chi_at(prim_ref, e + 1, m)], axis=0)
        flat = 1.0 - jnp.maximum(jnp.maximum(chi[:-4], chi[2:-2]), chi[4:])
        chi_ref[0] = chi[-4:-2]
        chi_ref[1] = chi[-2:]
        lower, upper = [], []
        for f in range(5):
            q = [planes(prim_ref, f, e + k, m) for k in (-1, 0, 1, 2)]
            d = q[2] - q[1]
            b = face_offset(q[1] - q[0], d, q[3] - q[2])
            a = d - b
            low, high = edges(q[1], shifted(a_ref[f], a), b, flat)
            a_ref[f] = a[-2:]
            lower.append(low)
            upper.append(high)
        return lower, upper

    def face(prim_ref, e, m):
        lower, upper = cell(prim_ref, e, m)
        flux = riemann([shifted(up_ref[f], upper[f]) for f in range(5)], lower, 1)
        for f in range(5):
            up_ref[f] = upper[f][-2:]
        return flux

    def begin_x(prim_ref):
        for f in range(5):
            q = [prim_ref[f, k] for k in (1, 2, 3, 4)]
            d = q[2] - q[1]
            a_ref[f] = d - face_offset(q[1] - q[0], d, q[3] - q[2])
        chi_ref[0] = chi_at(prim_ref, 2, 1)
        chi_ref[1] = chi_at(prim_ref, 3, 1)
        _, upper = cell(prim_ref, 3, 1)
        for f in range(5):
            up_ref[f] = upper[f]
        flux = face(prim_ref, GHOST, 1)
        for f in range(5):
            flux_ref[f] = flux[f]

    def rate_x(prim_ref, rest_ref, x, m):
        flux = face(prim_ref, x + GHOST + 1, m)
        rate = []
        for f in range(5):
            change = flux[f] - shifted(flux_ref[f], flux[f]) + planes(rest_ref, f, x, m)
            rate.append(ratio_ref[...] * change)
            flux_ref[f] = flux[f][-2:]
        return rate

    def first_x(x):
        rate = rate_x(q_ref, t_ref, x, XSTEP)
        for f in range(5):
            put(first_ref, f, x, XSTEP, planes(u_ref, f, x, XSTEP) - rate[f])

    def last_x(x):
        rate = rate_x(q_two_ref, t_two_ref, x, LAST_XSTEP)
        for f in range(5):
            new = 0.5 * (planes(u_ref, f, x, LAST_XSTEP) + (planes(first_ref, f, x, LAST_XSTEP) - rate[f]))
            for k in range(LAST_XSTEP):
                zero, one = by_slot(new[2 * k : 2 * k + 2])
                out_ref[0, f, x + k] = zero
                out_ref[1, f, x + k] = one

    arrive(0)
    arrive(1)
    pl.loop(0, GHOST)(lambda j: incoming(lax.rem(2 * j + depth - GHOST, depth)))
    send_edge(0, 1, u_ref)
    send_edge(0, 0, u_ref)

    def middle(c):
        arrive(c + 1)
        pl.loop(0, GHOST // 2)(lambda k: incoming(c * GHOST + 2 * k))

    middle(1)
    take_ghosts(0, 0, u_ref)
    begin_x(q_ref)
    pl.loop(0, GHOST, step=XSTEP)(first_x)

    @pl.loop(2, chunks - 1)
    def _(c):
        middle(c)

        @pl.loop(c * GHOST - GHOST, c * GHOST, step=XSTEP)
        def _(x):
            first_x(x)
            second(x - GHOST)

    send_edge(1, 0, first_ref)
    take_ghosts(0, 1, u_ref)
    pl.loop(depth - 2 * GHOST, depth, step=XSTEP)(first_x)
    send_edge(1, 1, first_ref)
    pl.loop(depth - 3 * GHOST, depth, step=2)(second)
    take_ghosts(1, 0, first_ref)
    take_ghosts(1, 1, first_ref)
    begin_x(q_two_ref)
    pl.loop(0, depth, step=LAST_XSTEP)(last_x)


def body(cell_state, swap_slots, neighbours):
    slots, fields, depth, _ = cell_state.shape
    n = lax.axis_size("box")
    rounds = n.bit_length() - 1
    cells = cell_state.reshape(slots, fields, depth, 8, 128)
    vmem, smem = (pl.BlockSpec(memory_space=space) for space in (pltpu.VMEM, pltpu.SMEM))
    pair = (slots, 8, 128)
    tile = (8, 128)
    scratch = [
        (fields, depth) + pair,
        (fields, depth) + pair,
        (fields, depth + 2 * GHOST) + pair,
        (fields, depth) + pair,
        (fields, depth + 2 * GHOST) + pair,
        (fields, depth) + pair,
        (fields,) + pair,
        (2,) + pair,
        (fields,) + pair,
        (fields,) + pair,
        tile,
        (depth, fields) + tile,
        (depth, fields) + tile,
        (rounds + 1,) + tile,
        (rounds,) + tile,
        (4, slots, GHOST, fields) + tile,
        (4, slots, GHOST, fields) + tile,
    ]
    counts = [depth // GHOST] * 2 + [rounds] * 2 + [4] * 2
    new = pl.pallas_call(
        functools.partial(step_kernel, n),
        out_shape=jax.ShapeDtypeStruct(cells.shape, jnp.float32),
        in_specs=[smem, smem, vmem],
        out_specs=vmem,
        scratch_shapes=[pltpu.VMEM(s, jnp.float32) for s in scratch]
        + [pltpu.SemaphoreType.DMA((k,)) for k in counts],
        compiler_params=pltpu.CompilerParams(
            vmem_limit_bytes=40 * 2**20, collective_id=0, has_side_effects=True
        ),
    )(swap_slots, neighbours, cells)
    return new.reshape(cell_state.shape)


def solution(mesh):
    in_specs = (P("box", None, None, None), P("box"), P("box", None))
    out_specs = P("box", None, None, None)
    return jax.shard_map(body, mesh=mesh, in_specs=in_specs, out_specs=out_specs, check_vma=False)
```

```python
import functools

import jax
import jax.numpy as jnp
from jax import lax
from jax.experimental import pallas as pl
from jax.experimental.pallas import tpu as pltpu
from jax.sharding import PartitionSpec as P

BZC = 32
GHOST = 4
RIEMANN_ITERS = 3
COURANT = 0.4
XSTEP = 2
IN_FLIGHT = 2
LAST_XSTEP = 4


def rcp(x):
    return pl.reciprocal(x, approx=True)


def primitives(u):
    density = jnp.maximum(u[0], 0.05)
    inv = 1.0 / density
    v1, v2, v3 = u[1] * inv, u[2] * inv, u[3] * inv
    internal = jnp.maximum(u[4] * inv - 0.5 * (v1 * v1 + v2 * v2 + v3 * v3), 0.05)
    pressure = density * (0.4 * internal + 0.1 * density)
    return density, v1, v2, v3, pressure


def signal_speed(q):
    sound = jnp.sqrt(0.1 * q[0] + 1.4 * q[4] / q[0])
    return jnp.abs(q[1]) + jnp.abs(q[2]) + jnp.abs(q[3]) + 3.0 * sound


def clip_to(x, span):
    return jnp.minimum(jnp.maximum(x, jnp.minimum(span, 0.0)), jnp.maximum(span, 0.0))


def face_offset(d_low, d, d_high):
    return clip_to(0.5 * d + (d_low - d_high) * (1.0 / 12.0), d)


def shock(near, far, far_sum, squeeze):
    steep = jnp.abs(near) * rcp(jnp.abs(far) + 0.1 * far_sum)
    squeeze = jnp.maximum(squeeze, 0.0)
    return jnp.clip(4.0 * steep - 3.0, 0.0, 1.0) * squeeze * rcp(squeeze + 0.2)


def edges(q, a, b, flat):
    lower = q - flat * clip_to(b + b, a)
    upper = q + flat * clip_to(a + a, b)
    return lower, upper


def wave_side(r, p):
    t = 0.1 * r * r
    c2 = r * (t + 1.4 * p)
    slope = 0.5 * r * (2.4 + t * rcp(p))
    return c2, slope, c2 - slope * p


def riemann(left, right, axis):
    r_l, u_l, p_l = left[0], left[axis], left[4]
    r_r, u_r, p_r = right[0], right[axis], right[4]
    c2_l, b_l, a_l = wave_side(r_l, p_l)
    c2_r, b_r, a_r = wave_side(r_r, p_r)
    c_l = c2_l * lax.rsqrt(c2_l)
    c_r = c2_r * lax.rsqrt(c2_r)
    floor_p = 0.1 * jnp.minimum(p_l, p_r)
    guess = (c_r * p_l + c_l * p_r + c_l * c_r * (u_l - u_r)) * rcp(c_l + c_r)
    guess = jnp.maximum(guess, floor_p)
    apart = u_r - u_l
    half_l, half_r = 0.5 * c2_l, 0.5 * c2_r
    for _ in range(RIEMANN_ITERS):
        i_l = lax.rsqrt(a_l + b_l * guess)
        i_r = lax.rsqrt(a_r + b_r * guess)
        gap = apart + (guess - p_r) * i_r + (guess - p_l) * i_l
        y_l = i_l * (0.5 + half_l * (i_l * i_l))
        y_r = i_r * (0.5 + half_r * (i_r * i_r))
        guess = jnp.maximum(guess - gap * rcp(y_l + y_r), floor_p)
    w2_l = a_l + b_l * guess
    w2_r = a_r + b_r * guess
    w_l = w2_l * lax.rsqrt(w2_l)
    w_r = w2_r * lax.rsqrt(w2_r)
    u = (w_l * u_l + w_r * u_r + (p_l - p_r)) * rcp(w_l + w_r)
    upwind = u >= 0.0
    pick = lambda x, y: jnp.where(upwind, x, y)
    r, p, w2 = pick(r_l, r_r), pick(p_l, p_r), pick(w2_l, w2_r)
    inv_r = rcp(r)
    internal = jnp.maximum(2.5 * p * inv_r - 0.25 * r, 0.05)
    drop = (guess - p) * rcp(w2)
    inner = jnp.maximum(internal + 0.5 * (guess + p) * drop, 0.1 * internal)
    mass = u * rcp(inv_r - drop)
    kinetic = u * u
    momenta = []
    for component in (1, 2, 3):
        if component == axis:
            momenta.append(mass * u + guess)
        else:
            carried = pick(left[component], right[component])
            kinetic = kinetic + carried * carried
            momenta.append(mass * carried)
    return [mass] + momenta + [mass * (inner + 0.5 * kinetic) + u * guess]


def z_shift(shape):
    z = lax.broadcasted_iota(jnp.int32, shape, 2) & (BZC - 1)
    keep = {1: z < BZC - 1, -1: z >= 1, -2: z >= 2}

    def shift(x, n):
        inside = pltpu.roll(x, (-n) % 128, 2)
        around = pltpu.roll(x, ((BZC if n > 0 else -BZC) - n) % 128, 2)
        return jnp.where(keep[n], inside, around)

    return shift


def y_shift(shape):
    lane = lax.broadcasted_iota(jnp.int32, shape, 2)
    row = lax.broadcasted_iota(jnp.int32, shape, 1)
    keep = {1: lane < 128 - BZC, -1: lane >= BZC, -2: lane >= 2 * BZC}
    first, last = row == 0, row == 7

    def shift(x, n):
        turned = pltpu.roll(x, (-n * BZC) % 128, 2)
        moved = pltpu.roll(turned, 7 if n > 0 else 1, 1)
        other = jnp.concatenate([moved[i ^ 1][None] for i in range(shape[0])], axis=0)
        carry = jnp.where(last if n > 0 else first, other, moved)
        return jnp.where(keep[n], turned, carry)

    return shift


def plane_sweep(q, shift_of, axis):
    shift = shift_of(q[0].shape)
    d = [shift(x, 1) - x for x in q]
    d_low = [shift(x, -1) for x in d]
    d_high = [shift(x, 1) for x in d]
    b = [face_offset(l, m, h) for l, m, h in zip(d_low, d, d_high)]
    a = [shift(m - x, -1) for m, x in zip(d, b)]
    p_high = q[4] + (d[4] + d_high[4])
    p_low = shift(q[4], -2)
    chi = shock(d[4] + d_low[4], p_high - p_low, p_high + p_low, -(d[axis] + d_low[axis]))
    flat = 1.0 - jnp.maximum(jnp.maximum(shift(chi, -1), chi), shift(chi, 1))
    pairs = [edges(*x, flat) for x in zip(q, a, b)]
    flux = riemann([shift(x[1], -1) for x in pairs], [x[0] for x in pairs], axis)
    return [shift(x, 1) - x for x in flux]


def step_kernel(
    n, swap_ref, next_ref, cell_ref, out_ref,
    u_ref, first_ref, q_ref, t_ref, q_two_ref, t_two_ref, a_ref, chi_ref, up_ref, flux_ref, ratio_ref,
    sent_ref, came_ref, fast_ref, fast_in_ref, edge_ref, ghost_ref,
    swap_send, swap_recv, fast_send, fast_recv, edge_send, edge_recv,
):
    depth = out_ref.shape[2]
    chunks = depth // GHOST
    rounds = n.bit_length() - 1
    me = lax.axis_index("box")
    right, left = lax.rem(me + 1, n), lax.rem(me + n - 1, n)
    peers = [me + 2**k * (1 - 2 * lax.rem(lax.div(me, 2**k), 2)) for k in range(rounds)]
    sent_slot = swap_ref[0]
    kept_slot = 1 - sent_slot

    barrier = pltpu.get_barrier_semaphore()
    for peer in peers + [left, right]:
        pl.semaphore_signal(barrier, inc=1, device_id=(peer,), device_id_type=pl.DeviceIdType.MESH)
    pl.semaphore_wait(barrier, rounds + 2)

    def remote(src, dst, send, recv, peer):
        return pltpu.make_async_remote_copy(
            src_ref=src, dst_ref=dst, send_sem=send, recv_sem=recv,
            device_id=(peer,), device_id_type=pl.DeviceIdType.MESH,
        )

    def swap_copy(c):
        part = pl.ds(c * GHOST, GHOST)
        return remote(sent_ref.at[part], came_ref.at[part], swap_send.at[c], swap_recv.at[c], peers[-1])

    def fast_copy(k):
        return remote(fast_ref.at[k], fast_in_ref.at[k], fast_send.at[k], fast_recv.at[k], peers[k])

    def edge_copy(stage, side):
        i = 2 * stage + side
        return remote(edge_ref.at[i], ghost_ref.at[i], edge_send.at[i], edge_recv.at[i], (left, right)[side])

    def chunk(j):
        return lax.rem(j + chunks - 1, chunks)

    def launch(j):
        c = chunk(j)
        for k in range(GHOST):
            x = c * GHOST + k
            for f in range(5):
                sent_ref[x, f] = cell_ref[sent_slot, f, x]
        swap_copy(c).start()

    def arrive(j):
        swap_copy(chunk(j)).wait()

        @pl.when(j + IN_FLIGHT < chunks)
        def _():
            launch(j + IN_FLIGHT)

    pl.loop(0, IN_FLIGHT)(launch)
    fast_ref[0] = jnp.zeros_like(fast_ref[0])

    @pl.loop(0, chunks)
    def _(c):
        speed = signal_speed(primitives([cell_ref[:, f, pl.ds(c * GHOST, GHOST)] for f in range(5)]))
        fast_ref[0] = jnp.maximum(fast_ref[0], jnp.max(speed, axis=(0, 1)))

    def kept(c):
        x = c * GHOST
        u = [cell_ref[kept_slot, f, pl.ds(x, GHOST)] for f in range(5)]
        q = primitives(u)
        dz = plane_sweep(q, z_shift, 3)
        for f in range(5):
            for k in range(GHOST):
                u_ref[f, x + k, 0] = u[f][k]
                q_ref[f, x + GHOST + k, 0] = q[f][k]
                t_ref[f, x + k, 0] = dz[f][k]

    for k in range(rounds):
        fast_copy(k).start()
        pl.loop(chunks * k // rounds, chunks * (k + 1) // rounds)(kept)
        fast_copy(k).wait()
        fast_ref[k + 1] = jnp.maximum(fast_ref[k], fast_in_ref[k])
    ratio_ref[...] = jnp.zeros_like(ratio_ref) + COURANT / jnp.max(fast_ref[rounds], keepdims=True)

    def planes(ref, f, x, m):
        return ref[f, pl.ds(x, m)].reshape(2 * m, 8, 128)

    def put(ref, f, x, m, value):
        ref[f, pl.ds(x, m)] = value.reshape(m, 2, 8, 128)

    def incoming(x):
        u = [came_ref[pl.ds(x, 2), f] for f in range(5)]
        q = primitives(u)
        for f in range(5):
            for k in range(2):
                u_ref[f, x + k, 1] = u[f][k]
                q_ref[f, x + GHOST + k, 1] = q[f][k]
        dz = plane_sweep(q, z_shift, 3)
        dy = plane_sweep([planes(q_ref, f, x + GHOST, 2) for f in range(5)], y_shift, 2)
        for f in range(5):
            along_z = [part[None] for k in range(2) for part in (t_ref[f, x + k, 0], dz[f][k])]
            put(t_ref, f, x, 2, dy[f] + jnp.concatenate(along_z, axis=0))

    def second(x):
        q = primitives([planes(first_ref, f, x, 2) for f in range(5)])
        for f in range(5):
            put(q_two_ref, f, x + GHOST, 2, q[f])
        dz = plane_sweep(q, z_shift, 3)
        dy = plane_sweep(q, y_shift, 2)
        for f in range(5):
            put(t_two_ref, f, x, 2, dz[f] + dy[f])

    def by_slot(pair):
        return jnp.where(sent_slot == 0, pair[1], pair[0]), jnp.where(sent_slot == 0, pair[0], pair[1])

    def send_edge(stage, side, source_ref):
        @pl.loop(0, GHOST)
        def _(k):
            for f in range(5):
                zero, one = by_slot(source_ref[f, k + side * (depth - GHOST)])
                edge_ref[2 * stage + side, 0, k, f] = zero
                edge_ref[2 * stage + side, 1, k, f] = one

        edge_copy(stage, side).start()

    prim_refs = (q_ref, q_two_ref)

    def take_ghosts(stage, side, source_ref):
        edge_copy(stage, 1 - side).wait()
        beside = [next_ref[slot, side] for slot in (kept_slot, sent_slot)]
        base = (left, right)[side] * 2
        own = side * (depth - 1)

        @pl.loop(0, GHOST)
        def _(k):
            u = []
            for f in range(5):
                mine = source_ref[f, own]
                parts = []
                for role in range(2):
                    zero, one = (ghost_ref[2 * stage + 1 - side, slot, k, f] for slot in range(2))
                    theirs = jnp.where(beside[role] == base, zero, one)
                    parts.append(jnp.where(beside[role] < 0, mine[role], theirs)[None])
                u.append(jnp.concatenate(parts, axis=0))
            q = primitives(u)
            for f in range(5):
                prim_refs[stage][f, k + side * (depth + GHOST)] = q[f]

    def chi_at(prim_ref, e, m):
        p = [planes(prim_ref, 4, e + k, m) for k in (-2, -1, 1, 2)]
        v = [planes(prim_ref, 1, e + k, m) for k in (-1, 1)]
        return shock(p[2] - p[1], p[3] - p[0], p[3] + p[0], v[0] - v[1])

    def shifted(first, rest):
        return first if rest.shape[0] == 2 else jnp.concatenate([first, rest[:-2]], axis=0)

    def cell(prim_ref, e, m):
        chi = jnp.concatenate([chi_ref[0], chi_ref[1], chi_at(prim_ref, e + 1, m)], axis=0)
        flat = 1.0 - jnp.maximum(jnp.maximum(chi[:-4], chi[2:-2]), chi[4:])
        chi_ref[0] = chi[-4:-2]
        chi_ref[1] = chi[-2:]
        lower, upper = [], []
        for f in range(5):
            q = [planes(prim_ref, f, e + k, m) for k in (-1, 0, 1, 2)]
            d = q[2] - q[1]
            b = face_offset(q[1] - q[0], d, q[3] - q[2])
            a = d - b
            low, high = edges(q[1], shifted(a_ref[f], a), b, flat)
            a_ref[f] = a[-2:]
            lower.append(low)
            upper.append(high)
        return lower, upper

    def face(prim_ref, e, m):
        lower, upper = cell(prim_ref, e, m)
        flux = riemann([shifted(up_ref[f], upper[f]) for f in range(5)], lower, 1)
        for f in range(5):
            up_ref[f] = upper[f][-2:]
        return flux

    def begin_x(prim_ref):
        for f in range(5):
            q = [prim_ref[f, k] for k in (1, 2, 3, 4)]
            d = q[2] - q[1]
            a_ref[f] = d - face_offset(q[1] - q[0], d, q[3] - q[2])
        chi_ref[0] = chi_at(prim_ref, 2, 1)
        chi_ref[1] = chi_at(prim_ref, 3, 1)
        _, upper = cell(prim_ref, 3, 1)
        for f in range(5):
            up_ref[f] = upper[f]
        flux = face(prim_ref, GHOST, 1)
        for f in range(5):
            flux_ref[f] = flux[f]

    def rate_x(prim_ref, rest_ref, x, m):
        flux = face(prim_ref, x + GHOST + 1, m)
        rate = []
        for f in range(5):
            change = flux[f] - shifted(flux_ref[f], flux[f]) + planes(rest_ref, f, x, m)
            rate.append(ratio_ref[...] * change)
            flux_ref[f] = flux[f][-2:]
        return rate

    def first_x(x):
        rate = rate_x(q_ref, t_ref, x, XSTEP)
        for f in range(5):
            put(first_ref, f, x, XSTEP, planes(u_ref, f, x, XSTEP) - rate[f])

    def last_x(x):
        rate = rate_x(q_two_ref, t_two_ref, x, LAST_XSTEP)
        for f in range(5):
            new = 0.5 * (planes(u_ref, f, x, LAST_XSTEP) + (planes(first_ref, f, x, LAST_XSTEP) - rate[f]))
            for k in range(LAST_XSTEP):
                zero, one = by_slot(new[2 * k : 2 * k + 2])
                out_ref[0, f, x + k] = zero
                out_ref[1, f, x + k] = one

    arrive(0)
    arrive(1)
    pl.loop(0, GHOST)(lambda j: incoming(lax.rem(2 * j + depth - GHOST, depth)))
    send_edge(0, 1, u_ref)
    send_edge(0, 0, u_ref)

    def middle(c):
        arrive(c + 1)
        pl.loop(0, GHOST // 2)(lambda k: incoming(c * GHOST + 2 * k))

    middle(1)
    take_ghosts(0, 0, u_ref)
    begin_x(q_ref)
    pl.loop(0, GHOST, step=XSTEP)(first_x)

    @pl.loop(2, chunks - 1)
    def _(c):
        middle(c)

        @pl.loop(c * GHOST - GHOST, c * GHOST, step=XSTEP)
        def _(x):
            first_x(x)
            second(x - GHOST)

    send_edge(1, 0, first_ref)
    take_ghosts(0, 1, u_ref)
    pl.loop(depth - 2 * GHOST, depth, step=XSTEP)(first_x)
    send_edge(1, 1, first_ref)
    pl.loop(depth - 3 * GHOST, depth, step=2)(second)
    take_ghosts(1, 0, first_ref)
    take_ghosts(1, 1, first_ref)
    begin_x(q_two_ref)
    pl.loop(0, depth, step=LAST_XSTEP)(last_x)


def body(cell_state, swap_slots, neighbours):
    slots, fields, depth, _ = cell_state.shape
    n = lax.axis_size("box")
    rounds = n.bit_length() - 1
    cells = cell_state.reshape(slots, fields, depth, 8, 128)
    vmem, smem = (pl.BlockSpec(memory_space=space) for space in (pltpu.VMEM, pltpu.SMEM))
    pair = (slots, 8, 128)
    tile = (8, 128)
    scratch = [
        (fields, depth) + pair,
        (fields, depth) + pair,
        (fields, depth + 2 * GHOST) + pair,
        (fields, depth) + pair,
        (fields, depth + 2 * GHOST) + pair,
        (fields, depth) + pair,
        (fields,) + pair,
        (2,) + pair,
        (fields,) + pair,
        (fields,) + pair,
        tile,
        (depth, fields) + tile,
        (depth, fields) + tile,
        (rounds + 1,) + tile,
        (rounds,) + tile,
        (4, slots, GHOST, fields) + tile,
        (4, slots, GHOST, fields) + tile,
    ]
    counts = [depth // GHOST] * 2 + [rounds] * 2 + [4] * 2
    new = pl.pallas_call(
        functools.partial(step_kernel, n),
        out_shape=jax.ShapeDtypeStruct(cells.shape, jnp.float32),
        in_specs=[smem, smem, vmem],
        out_specs=vmem,
        scratch_shapes=[pltpu.VMEM(s, jnp.float32) for s in scratch]
        + [pltpu.SemaphoreType.DMA((k,)) for k in counts],
        compiler_params=pltpu.CompilerParams(
            vmem_limit_bytes=40 * 2**20, collective_id=0, has_side_effects=True
        ),
    )(swap_slots, neighbours, cells)
    return new.reshape(cell_state.shape)


def solution(mesh):
    in_specs = (P("box", None, None, None), P("box"), P("box", None))
    out_specs = P("box", None, None, None)
    return jax.shard_map(body, mesh=mesh, in_specs=in_specs, out_specs=out_specs, check_vma=False)
```
